512 devices in a mesh: ctx: 16 (over z, core), head: 8 (over y), dp: 4 (over x).
Axes of the slice: x: 4, y: 8, z: 8, core: 2. Of those that a mesh axis runs over, the one named last changes fastest.
Arguments:
- positions: int32 [4, 2048], P('dp', 'ctx'), may hold values from 0 to 2047, as said below
- unnormed_latent: bfloat16 [4, 2048, 512], P('dp', 'ctx'), may hold values from -6 to 6
- latent_norm_gain: float32 [512], replicated, may hold values from 0.5 to 1.5
- key_rope: bfloat16 [4, 2048, 64], P('dp', 'ctx'), may hold values from -9 to 9
- query_nope: bfloat16 [4, 2048, 8192], P('dp', 'ctx', 'head'), may hold values from -6 to 6
- query_rope: bfloat16 [4, 2048, 4096], P('dp', 'ctx', 'head'), may hold values from -48 to 48
- key_up: bfloat16 [64, 128, 512], P('head'), may hold values from -0.5 to 0.5
- value_up: bfloat16 [64, 128, 512], P('head'), may hold values from -0.5 to 0.5
- grad_out: bfloat16 [4, 2048, 8192], P('dp', 'ctx', 'head'), may hold values from -0.75 to 0.75
Outputs:
- raw_latent_gradient: float32 [4, 2048, 512], P('dp', ('ctx', 'head'))
- rope_grad: float32 [4, 2048, 64], P('dp', ('ctx', 'head'))
- norm_gain_gradient: float32 [512], replicated
The draws below stay inside these ranges and needn't reach their ends.
Inputs may be any that keep to these rules, and one draw needn't show every extreme that they name: In each sequence every position 0 to 2047 stands once. The 128 rows of one index of ctx are two runs of 64 consecutive positions in increasing order: the first starts at 64 * j for some j below 16, the second at 2048 - 64 * (j + 1); which j falls to which index is drawn.
All inputs are finite; a program needn't handle non-finite values.
Results may differ from the reference program's by a relative error of at most 0.04.
Values may be sent and summed in bfloat16 or wider, within the bound.
A program may use at most 64 MiB of HBM per device.

```python
import math
import jax
import jax.numpy as jnp
from jax import lax

LAT = 512
ROPE = 64
HD = 128
VD = 128
H_DEV = 8
TOK_DEV = 128
HEADS = 64
SEQUENCE_LENGTH = 2048
BATCH_SEQUENCES = 4
N_CTX = 16


def draw_positions(key, part):
    key = jax.random.fold_in(key, 7)
    shards = SEQUENCE_LENGTH // TOK_DEV
    half = TOK_DEV // 2
    seq_keys = jax.random.split(key, BATCH_SEQUENCES)
    pairs = jax.vmap(lambda one: jax.random.permutation(one, shards))(seq_keys).astype(jnp.int32)
    offsets = jnp.arange(half, dtype=jnp.int32)
    lower = pairs[:, :, None] * half + offsets
    upper = (2 * shards - 1 - pairs)[:, :, None] * half + offsets
    return jnp.concatenate([lower, upper], axis=2).reshape(BATCH_SEQUENCES, SEQUENCE_LENGTH).astype(jnp.int32)


def draw_key_rope(key, part):
    key = jax.random.fold_in(key, 11)
    base = jax.random.normal(key, (BATCH_SEQUENCES, SEQUENCE_LENGTH, ROPE), jnp.float32)
    return base.astype(jnp.bfloat16)


def draw_query_rope(key, part):
    key = jax.random.fold_in(key, 13)
    heads = HEADS
    base = jax.random.normal(key, (BATCH_SEQUENCES, SEQUENCE_LENGTH, heads, ROPE), jnp.float32)
    return base.reshape(BATCH_SEQUENCES, SEQUENCE_LENGTH, heads * ROPE).astype(jnp.bfloat16)


def block_scale(key, shape, cuts, least, largest):
    def one(position, parts):
        steps = jax.random.uniform(jax.random.fold_in(jax.random.fold_in(key, 6), position), (parts,), jnp.float32, least / len(cuts), largest / len(cuts))
        return jnp.repeat(jnp.exp(steps), shape[position] // parts).reshape((-1,) + (1,) * (len(shape) - position - 1))

    factor_of = one(*cuts[0])
    for cut in cuts[1:]:
        factor_of = factor_of * one(*cut)
    return factor_of


def scatter_about(stream_key, extent, width, reach, cuts=(), kind=jnp.bfloat16):
    array = jax.random.normal(stream_key, extent, jnp.float32) * width
    if len(cuts) > 0:
        array = block_scale(stream_key, extent, cuts, -0.22, 0.18) * array
    return jnp.clip(array, min=-reach, max=reach).astype(kind)


def setup_inputs(seed: int = 0) -> dict:
    streams_of = jax.random.split(jax.random.key(seed), 10)
    positions = draw_positions(jax.random.fold_in(streams_of[9], 71), 0)
    unnormed_latent = scatter_about(streams_of[1], (BATCH_SEQUENCES, SEQUENCE_LENGTH, LAT), 1.0, 6.0, ((0, 4), (1, 16)))
    latent_norm_gain = jnp.clip(1.0 + 0.1 * jax.random.normal(streams_of[2], (LAT,), jnp.float32), 0.5, 1.5)
    key_rope = draw_key_rope(jax.random.fold_in(streams_of[9], 71), 0)
    query_nope = scatter_about(streams_of[4], (BATCH_SEQUENCES, SEQUENCE_LENGTH, HEADS * HD), 1.0, 6.0, ((0, 4), (1, 16), (2, 8)))
    query_rope = draw_query_rope(jax.random.fold_in(streams_of[9], 71), 0)
    key_up = scatter_about(streams_of[6], (HEADS, HD, LAT), HD ** -0.5, 0.5, ((0, 8),))
    value_up = scatter_about(streams_of[7], (HEADS, VD, LAT), VD ** -0.5, 0.5, ((0, 8),))
    grad_out = scatter_about(streams_of[8], (BATCH_SEQUENCES, SEQUENCE_LENGTH, HEADS * VD), 0.125, 0.75, ((0, 4), (1, 16), (2, 8)))
    return dict(positions=positions, unnormed_latent=unnormed_latent, latent_norm_gain=latent_norm_gain, key_rope=key_rope, query_nope=query_nope, query_rope=query_rope, key_up=key_up, value_up=value_up, grad_out=grad_out)


def apply_latent_norm(unnormed_latent, latent_norm_gain):
    unnormed_rows = unnormed_latent.astype(jnp.float32)
    root_mean_square = jnp.sqrt(lax.optimization_barrier(jnp.mean(unnormed_rows * unnormed_rows, axis=-1, keepdims=True)) + 1e-06)
    normalized_latent = unnormed_rows / root_mean_square
    return (normalized_latent, root_mean_square, (normalized_latent * latent_norm_gain).astype(jnp.bfloat16))

def sequence_terms(pos, latent_state, krope, qnope, qrope, key_up, value_up, gout):
    scale = float(HD + ROPE) ** (-0.5)
    heads = key_up.shape[0]
    groups = heads // H_DEV
    qn = qnope.reshape(SEQUENCE_LENGTH, heads, HD)
    qr = qrope.reshape(SEQUENCE_LENGTH, heads, ROPE)
    go = gout.reshape(SEQUENCE_LENGTH, heads, VD)
    visible = pos[None, :] <= pos[:, None]

    def one_head(carry, index):
        lat_acc, rope_acc = carry
        q_head = lax.dynamic_index_in_dim(qn, index, 1, keepdims=False)
        r_head = lax.dynamic_index_in_dim(qr, index, 1, keepdims=False)
        g_head = lax.dynamic_index_in_dim(go, index, 1, keepdims=False)
        k_mat = lax.dynamic_index_in_dim(key_up, index, 0, keepdims=False)
        v_mat = lax.dynamic_index_in_dim(value_up, index, 0, keepdims=False)
        qlat = jnp.dot(q_head, k_mat, preferred_element_type=jnp.float32).astype(jnp.bfloat16)
        olat = jnp.dot(g_head, v_mat, preferred_element_type=jnp.float32).astype(jnp.bfloat16)
        scores = jnp.dot(qlat, latent_state.T, preferred_element_type=jnp.float32)
        scores = scores + jnp.dot(r_head, krope.T, preferred_element_type=jnp.float32)
        scores = jnp.where(visible, scores * scale, -jnp.inf)
        top = lax.optimization_barrier(jnp.max(scores, axis=1, keepdims=True))
        weights = jnp.exp(scores - top)
        probs = weights / lax.optimization_barrier(jnp.sum(weights, axis=1, keepdims=True))
        dprob = jnp.dot(olat, latent_state.T, preferred_element_type=jnp.float32)
        delta = lax.optimization_barrier(jnp.sum(probs * dprob, axis=1, keepdims=True))
        dscore = probs * (dprob - delta) * scale
        probs_b = probs.astype(jnp.bfloat16).astype(jnp.float32).reshape(N_CTX, TOK_DEV, SEQUENCE_LENGTH)
        dscore_b = dscore.astype(jnp.bfloat16).astype(jnp.float32).reshape(N_CTX, TOK_DEV, SEQUENCE_LENGTH)
        olat_s = olat.astype(jnp.float32).reshape(N_CTX, TOK_DEV, LAT)
        qlat_s = qlat.astype(jnp.float32).reshape(N_CTX, TOK_DEV, LAT)
        r_s = r_head.astype(jnp.float32).reshape(N_CTX, TOK_DEV, ROPE)
        lat_acc = lat_acc + jnp.einsum('cqk,cql->ckl', probs_b, olat_s) + jnp.einsum('cqk,cql->ckl', dscore_b, qlat_s)
        rope_acc = rope_acc + jnp.einsum('cqk,cqr->ckr', dscore_b, r_s)
        return ((lat_acc, rope_acc), None)

    def one_group(group):
        start = jnp.zeros((H_DEV,), jnp.int32) + group.astype(jnp.int32) * H_DEV + jnp.arange(H_DEV, dtype=jnp.int32)
        empty = (jnp.zeros((N_CTX, SEQUENCE_LENGTH, LAT), jnp.float32), jnp.zeros((N_CTX, SEQUENCE_LENGTH, ROPE), jnp.float32))
        (lat_acc, rope_acc), _ = lax.scan(one_head, empty, start)
        lat_sum = lax.optimization_barrier(jnp.sum(lat_acc.astype(jnp.bfloat16).astype(jnp.float32), axis=0))
        rope_sum = lax.optimization_barrier(jnp.sum(rope_acc.astype(jnp.bfloat16).astype(jnp.float32), axis=0))
        return (lat_sum, rope_sum)
    lat_groups, rope_groups = lax.map(one_group, jnp.arange(groups, dtype=jnp.int32))
    return (lax.optimization_barrier(jnp.sum(lat_groups, axis=0)), lax.optimization_barrier(jnp.sum(rope_groups, axis=0)))

def reference(positions, unnormed_latent, latent_norm_gain, key_rope, query_nope, query_rope, key_up, value_up, grad_out):
    normalized_latent, root_mean_square, latent_state = apply_latent_norm(unnormed_latent, latent_norm_gain)
    lat_list = []
    rope_list = []
    for seq in range(BATCH_SEQUENCES):
        lat_cot, rope_cot = sequence_terms(positions[seq], latent_state[seq], key_rope[seq], query_nope[seq], query_rope[seq], key_up, value_up, grad_out[seq])
        lat_list.append(lat_cot)
        rope_list.append(rope_cot)
    latent_output_gradient = jnp.stack(lat_list, axis=0)
    rope_grad = jnp.stack(rope_list, axis=0)
    scaled_latent = latent_norm_gain * latent_output_gradient
    raw_latent_gradient = (scaled_latent - normalized_latent * lax.optimization_barrier(jnp.mean(scaled_latent * normalized_latent, axis=-1, keepdims=True))) / root_mean_square
    norm_gain_gradient = lax.optimization_barrier(jnp.sum(latent_output_gradient * normalized_latent, axis=(0, 1))) / math.sqrt(BATCH_SEQUENCES * SEQUENCE_LENGTH)
    return (raw_latent_gradient, rope_grad, norm_gain_gradient)
```

```python
import functools
import math

import jax
import jax.numpy as jnp
from jax import lax
from jax.experimental import pallas as pl
from jax.experimental.pallas import tpu as pltpu
from jax.sharding import PartitionSpec as P

BF16 = jnp.bfloat16
F32 = jnp.float32
MESH = pl.DeviceIdType.MESH


def dot(a, b):
    return jnp.dot(a, b, preferred_element_type=F32)


def dot_t(a, b):
    return lax.dot_general(a, b, (((1,), (1,)), ((), ())), preferred_element_type=F32)


def kernel(
    nz, ny, nx, total_rows,
    pos_ref, x_ref, gain_ref, kr_ref, qn_ref, qr_ref, ku_ref, vu_ref, go_ref,
    raw_ref, rope_ref, gout_ref,
    keys, posbuf, qlat, olat, qrp, wbuf, dbuf, diff,
    pown, psib, rsib, sendp, recvp, sendm, recvm, ysend, yrecv, gsend, gx, gy, gc,
    sem_as, sem_ar, sem_ps, sem_pr, sem_ss, sem_sr, sem_zs, sem_zr, sem_ys, sem_yr, sem_gs, sem_gr,
):
    nc = 2 * nz
    half_z = nz // 2
    me = lax.axis_index("ctx")
    y = lax.axis_index("head")
    x = lax.axis_index("dp")
    z = me // 2
    c = lax.rem(me, 2)
    sib = z * 2 + (1 - c)
    up = lax.rem(z + 1, nz) * 2 + c
    down = lax.rem(z + nz - 1, nz) * 2 + c

    def at_z(off):
        return lax.rem(z + off + nz, nz)

    def rem_copy(src, dst, ssem, rsem, dev):
        return pltpu.make_async_remote_copy(
            src_ref=src, dst_ref=dst, send_sem=ssem, recv_sem=rsem, device_id=dev, device_id_type=MESH
        )

    barrier = pltpu.get_barrier_semaphore()
    for d in range(1, nc):
        pl.semaphore_signal(barrier, inc=1, device_id={"ctx": lax.rem(me + d, nc)}, device_id_type=MESH)
    for d in range(1, ny):
        pl.semaphore_signal(barrier, inc=1, device_id={"head": lax.rem(y + d, ny)}, device_id_type=MESH)
    for d in range(1, nx):
        pl.semaphore_signal(barrier, inc=1, device_id={"dp": lax.rem(x + d, nx)}, device_id_type=MESH)

    rows = x_ref[0].astype(F32)
    rms = jnp.sqrt(jnp.mean(rows * rows, axis=-1, keepdims=True) + 1e-06)
    keys[me, 0:128, :] = (rows / rms * gain_ref[...]).astype(BF16)
    ri = lax.broadcasted_iota(jnp.int32, (64, 128), 0)
    ci = lax.broadcasted_iota(jnp.int32, (64, 128), 1)
    packed = dot(kr_ref[0, 0:64, :], (ci == ri).astype(BF16)) + dot(
        kr_ref[0, 64:128, :], (ci == ri + 64).astype(BF16)
    )
    packed = packed.astype(BF16)
    for g in range(4):
        keys[me, 128:144, 128 * g : 128 * g + 128] = packed[16 * g : 16 * g + 16]
    posbuf[me] = jnp.broadcast_to(pos_ref[...], (8, 128))

    pl.semaphore_wait(barrier, (nc - 1) + (ny - 1) + (nx - 1))

    started = []

    def start(copy):
        copy.start()
        started.append(copy)

    def gather_copy(block, way, index):
        dev = (up, down, sib)[way]
        return rem_copy(
            keys.at[block], keys.at[block], sem_as.at[way, index], sem_ar.at[way, index], {"ctx": dev}
        )

    def pos_copy(d, slot):
        return rem_copy(
            posbuf.at[slot], posbuf.at[slot], sem_ps.at[d], sem_pr.at[d], {"ctx": lax.rem(me + d, nc)}
        )

    start(gather_copy(me, 0, 1))
    if half_z > 1:
        start(gather_copy(me, 1, 1))
    start(gather_copy(me, 2, 0))
    for d in range(1, nc):
        start(pos_copy(d, me))

    fi = lax.broadcasted_iota(jnp.int32, (128, 128), 0)
    fj = lax.broadcasted_iota(jnp.int32, (128, 128), 1)
    for h in range(8):
        part = dot(qn_ref[0, :, 128 * h : 128 * h + 128], ku_ref[h]).astype(BF16)
        qlat[0, 64 * h : 64 * h + 64, :] = part[0:64]
        qlat[1, 64 * h : 64 * h + 64, :] = part[64:128]
        part = dot(go_ref[0, :, 128 * h : 128 * h + 128], vu_ref[h]).astype(BF16)
        olat[0, 64 * h : 64 * h + 64, :] = part[0:64]
        olat[1, 64 * h : 64 * h + 64, :] = part[64:128]
        pair = qr_ref[0, :, 128 * (h // 2) : 128 * (h // 2) + 128]
        e = 64 * (h % 2)
        left = dot(pair, ((fi == fj + e) & (fj < 64)).astype(BF16)).astype(BF16)
        right = dot(pair[64:128], ((fi + 64 - e == fj) & (fj >= 64)).astype(BF16)).astype(BF16)
        qrp[0, 64 * h : 64 * h + 64, :] = left[0:64]
        qrp[1, 64 * h : 64 * h + 64, :] = left[64:128]
        qrp[2, 64 * h : 64 * h + 64, :] = right
    diff[...] = lax.rem(lax.broadcasted_iota(jnp.int32, (64, 512), 1), 64) - lax.broadcasted_iota(
        jnp.int32, (64, 512), 0
    )

    scale = float(128 + 64) ** (-0.5)
    to_log2 = scale * math.log2(math.e)

    groups = [[0]] + [[t, -t] for t in range(1, half_z)] + [[half_z]]
    first = []
    count = 0
    for g in groups:
        first.append(count)
        count += 2 * len(g)

    def blocks_of(g):
        return [at_z(off) * 2 + cc for off in g for cc in range(2)]

    def cat(parts):
        return parts[0] if len(parts) == 1 else jnp.concatenate(parts, axis=0)

    def rope_rows(b):
        return [keys[b, 128:144, 128 * g : 128 * g + 128] for g in range(4)]

    m_up = jnp.full((1, 512), -jnp.inf, F32)
    m_lo = m_up
    l_up = jnp.zeros((1, 512), F32)
    l_lo, d_up, d_lo = l_up, l_up, l_up
    tops = []
    for t, g in enumerate(groups):
        if t == 0:
            for d in range(1, nc):
                pos_copy(d, lax.rem(me - d + nc, nc)).wait_recv()
        else:
            block = at_z(-t) * 2 + c
            gather_copy(block, 0, t).wait_recv()
            if t < half_z:
                start(gather_copy(block, 0, t + 1))
            start(gather_copy(block, 2, t))
            if t < half_z:
                block = at_z(t) * 2 + c
                gather_copy(block, 1, t).wait_recv()
                if t + 1 < half_z:
                    start(gather_copy(block, 1, t + 1))
                start(gather_copy(block, 2, half_z + t))
        other = 1 - c
        gather_copy(at_z(-t) * 2 + other, 2, t).wait_recv()
        if 0 < t < half_z:
            gather_copy(at_z(t) * 2 + other, 2, half_z + t).wait_recv()

        blocks = blocks_of(g)
        n = 64 * len(blocks)
        span = pl.ds(64 * first[t], n)
        low = cat([keys[b, 0:64, :] for b in blocks])
        high = cat([keys[b, 64:128, :] for b in blocks])
        rope = cat([r for b in blocks for r in rope_rows(b)])
        wbuf[0, span, :] = (dot_t(low, qlat[1]) + dot_t(rope, qrp[1])) * to_log2
        dbuf[0, span, :] = dot_t(low, olat[1])
        s_high = (dot_t(high, qlat[1]) + dot_t(rope, qrp[2])) * to_log2
        dbuf[1, span, :] = dot_t(high, olat[1])
        s_low = (dot_t(low, qlat[0]) + dot_t(rope, qrp[0])) * to_log2
        dbuf[2, span, :] = dot_t(low, olat[0])
        for i, b in enumerate(blocks):
            sub = pl.ds(64 * (first[t] + i), 64)
            late = posbuf[b, 0:1, 64:65] - pos_ref[0:1, 64:65]
            early = posbuf[b, 0:1, 0:1] - pos_ref[0:1, 0:1]
            wbuf[1, sub, :] = jnp.where(diff[...] >= late, s_high[64 * i : 64 * i + 64], -jnp.inf)
            wbuf[2, sub, :] = jnp.where(diff[...] >= early, s_low[64 * i : 64 * i + 64], -jnp.inf)
        new_up = jnp.maximum(
            m_up,
            jnp.maximum(
                jnp.max(wbuf[0, span, :], axis=0, keepdims=True), jnp.max(wbuf[1, span, :], axis=0, keepdims=True)
            ),
        )
        new_lo = jnp.maximum(m_lo, jnp.max(wbuf[2, span, :], axis=0, keepdims=True))
        a_up = jnp.exp2(m_up - new_up)
        a_lo = jnp.exp2(m_lo - new_lo)
        m_up, m_lo = new_up, new_lo
        l_up, d_up, l_lo, d_lo = l_up * a_up, d_up * a_up, l_lo * a_lo, d_lo * a_lo
        tops.append((m_up, m_lo))
        for kind in range(3):
            top = m_lo if kind == 2 else m_up
            w = jnp.exp2(wbuf[kind, span, :] - top)
            wbuf[kind, span, :] = w
            l_add = jnp.sum(w, axis=0, keepdims=True)
            d_add = jnp.sum(w * dbuf[kind, span, :], axis=0, keepdims=True)
            if kind == 2:
                l_lo, d_lo = l_lo + l_add, d_lo + d_add
            else:
                l_up, d_up = l_up + l_add, d_up + d_add

    inv_up, inv_lo = 1.0 / l_up, 1.0 / l_lo
    delta_up, delta_lo = d_up * inv_up, d_lo * inv_lo

    def sib_copy(index):
        return rem_copy(
            psib.at[index], rsib.at[index], sem_ss.at[index], sem_sr.at[index], {"ctx": sib}
        )

    def ring_copy(way, step):
        src, dst, dev = ((sendp, recvp, up), (sendm, recvm, down))[way]
        return rem_copy(
            src.at[step], dst.at[step], sem_zs.at[way, step], sem_zr.at[way, step], {"ctx": dev}
        )

    index_of = {off: i for i, off in enumerate(off for g in groups for off in g)}

    def summed(off):
        i = index_of[off]
        return pown[i].astype(F32) + rsib[i].astype(F32)

    def send_on(t):
        for off in groups[t]:
            sib_copy(index_of[off]).wait_recv()
        step = half_z - t
        total = summed(t)
        if step > 0:
            ring_copy(0, step - 1).wait_recv()
            total = total + recvp[step - 1].astype(F32)
        sendp[step] = total.astype(BF16)
        start(ring_copy(0, step))
        if t < half_z:
            step = half_z - 1 - t
            total = summed(-t)
            if step > 0:
                ring_copy(1, step - 1).wait_recv()
                total = total + recvm[step - 1].astype(F32)
            sendm[step] = total.astype(BF16)
            start(ring_copy(1, step))

    gain_acc = jnp.zeros((1, 512), F32)
    for t in reversed(range(len(groups))):
        g = groups[t]
        blocks = blocks_of(g)
        n = 64 * len(blocks)
        span = pl.ds(64 * first[t], n)
        c_up = jnp.exp2(tops[t][0] - m_up) * inv_up
        c_lo = jnp.exp2(tops[t][1] - m_lo) * inv_lo
        probs = []
        dscores = []
        for kind in range(3):
            factor, delta = (c_lo, delta_lo) if kind == 2 else (c_up, delta_up)
            p = wbuf[kind, span, :] * factor
            probs.append(p.astype(BF16))
            dscores.append((p * (dbuf[kind, span, :] - delta) * scale).astype(BF16))
        lat_low = (
            dot(probs[0], olat[1]) + dot(dscores[0], qlat[1]) + dot(probs[2], olat[0]) + dot(dscores[2], qlat[0])
        )
        lat_high = dot(probs[1], olat[1]) + dot(dscores[1], qlat[1])
        rope = dot(dscores[0], qrp[1]) + dot(dscores[1], qrp[2]) + dot(dscores[2], qrp[0])
        low = cat([keys[b, 0:64, :] for b in blocks])
        high = cat([keys[b, 64:128, :] for b in blocks])
        gain_acc = gain_acc + jnp.sum(
            lat_low * low.astype(F32) + lat_high * high.astype(F32), axis=0, keepdims=True
        )
        lat_low = lat_low.astype(BF16)
        lat_high = lat_high.astype(BF16)
        rope = rope.astype(BF16)
        for i, b in enumerate(blocks):
            index = index_of[g[i // 2]]

            def put(buf):
                buf[index, 0:64, :] = lat_low[64 * i : 64 * i + 64]
                buf[index, 64:128, :] = lat_high[64 * i : 64 * i + 64]
                for k in range(4):
                    buf[index, 128:144, 128 * k : 128 * k + 128] = rope[64 * i + 16 * k : 64 * i + 16 * k + 16]

            @pl.when(c == i % 2)
            def _():
                put(pown)

            @pl.when(c != i % 2)
            def _():
                put(psib)

        for off in g:
            start(sib_copy(index_of[off]))
        if t < half_z:
            send_on(t + 1)

    gsend[0] = gain_acc

    def gain_copy(stage, d, slot):
        buf, base, axis, pos, size = (
            (gx, 0, "dp", x, nx), (gy, nx - 1, "head", y, ny), (gc, nx + ny - 2, "ctx", me, nc)
        )[stage]
        return rem_copy(
            gsend.at[stage], buf.at[slot], sem_gs.at[base + d - 1], sem_gr.at[base + d - 1],
            {axis: lax.rem(pos + d, size)},
        )

    def gain_send(stage):
        buf, pos, size = ((gx, x, nx), (gy, y, ny), (gc, me, nc))[stage]
        buf[pos] = gsend[stage]
        for d in range(1, size):
            start(gain_copy(stage, d, pos))

    def gain_sum(stage):
        buf, pos, size = ((gx, x, nx), (gy, y, ny), (gc, me, nc))[stage]
        for d in range(1, size):
            gain_copy(stage, d, lax.rem(pos - d + size, size)).wait_recv()
        return jnp.sum(buf[...], axis=0)

    gain_send(0)
    gsend[1] = gain_sum(0)
    gain_send(1)

    sib_copy(0).wait_recv()
    total = summed(0)
    ring_copy(0, half_z - 1).wait_recv()
    total = total + recvp[half_z - 1].astype(F32)
    if half_z > 1:
        ring_copy(1, half_z - 2).wait_recv()
        total = total + recvm[half_z - 2].astype(F32)
    for k in range(ny):
        q = k % 4
        ysend[k, :, 0:512] = total[16 * k : 16 * k + 16, :].astype(BF16)
        ysend[k, :, 512:640] = total[128:144, 128 * q : 128 * q + 128].astype(BF16)

    def y_copy(d, slot):
        peer = lax.rem(y + d, ny)
        return rem_copy(
            ysend.at[peer], yrecv.at[slot], sem_ys.at[d - 1], sem_yr.at[d - 1], {"head": peer}
        )

    for d in range(1, ny):
        start(y_copy(d, y))
    yrecv[y] = ysend[y]
    gsend[2] = gain_sum(1)
    gain_send(2)
    for d in range(1, ny):
        y_copy(d, lax.rem(y - d + ny, ny)).wait_recv()
    mine = jnp.sum(yrecv[...].astype(F32), axis=0)

    cot = mine[:, 0:512]
    own = x_ref[0, pl.ds(pl.multiple_of(16 * y, 16), 16), :].astype(F32)
    own_rms = jnp.sqrt(jnp.mean(own * own, axis=-1, keepdims=True) + 1e-06)
    xhat = own / own_rms
    scaled = gain_ref[...] * cot
    raw_ref[0] = (scaled - xhat * jnp.mean(scaled * xhat, axis=-1, keepdims=True)) / own_rms
    both = mine[:, 512:640]
    rope_ref[0] = jnp.where(y >= ny // 2, pltpu.roll(both, 64, 1), both)[:, 0:64]

    gout_ref[...] = gain_sum(2) / gain_ref[...] * (1.0 / math.sqrt(total_rows))
    for copy in started:
        copy.wait_send()


def solution(mesh):
    nc, ny, nx = mesh.shape["ctx"], mesh.shape["head"], mesh.shape["dp"]
    nz = nc // 2
    half_z = nz // 2

    def per_device(pos, unnormed, gain, kr, qn, qr, ku, vu, go):
        dma = pltpu.SemaphoreType.DMA
        out = pl.pallas_call(
            functools.partial(kernel, nz, ny, nx, nc * 128 * nx),
            out_shape=(
                jax.ShapeDtypeStruct((1, 16, 512), F32),
                jax.ShapeDtypeStruct((1, 16, 64), F32),
                jax.ShapeDtypeStruct((1, 512), F32),
            ),
            in_specs=[pl.BlockSpec(memory_space=pltpu.VMEM)] * 9,
            out_specs=[pl.BlockSpec(memory_space=pltpu.VMEM)] * 3,
            scratch_shapes=[
                pltpu.VMEM((nc, 144, 512), BF16),
                pltpu.VMEM((nc, 8, 128), jnp.int32),
                pltpu.VMEM((2, 512, 512), BF16),
                pltpu.VMEM((2, 512, 512), BF16),
                pltpu.VMEM((3, 512, 128), BF16),
                pltpu.VMEM((3, 64 * nc, 512), F32),
                pltpu.VMEM((3, 64 * nc, 512), F32),
                pltpu.VMEM((64, 512), jnp.int32),
                pltpu.VMEM((nz, 144, 512), BF16),
                pltpu.VMEM((nz, 144, 512), BF16),
                pltpu.VMEM((nz, 144, 512), BF16),
                pltpu.VMEM((half_z, 144, 512), BF16),
                pltpu.VMEM((half_z, 144, 512), BF16),
                pltpu.VMEM((max(half_z - 1, 1), 144, 512), BF16),
                pltpu.VMEM((max(half_z - 1, 1), 144, 512), BF16),
                pltpu.VMEM((ny, 16, 640), BF16),
                pltpu.VMEM((ny, 16, 640), BF16),
                pltpu.VMEM((3, 1, 512), F32),
                pltpu.VMEM((nx, 1, 512), F32),
                pltpu.VMEM((ny, 1, 512), F32),
                pltpu.VMEM((nc, 1, 512), F32),
                dma((3, nz + 1)),
                dma((3, nz + 1)),
                dma((nc,)),
                dma((nc,)),
                dma((nz,)),
                dma((nz,)),
                dma((2, half_z)),
                dma((2, half_z)),
                dma((ny,)),
                dma((ny,)),
                dma((nx + ny + nc,)),
                dma((nx + ny + nc,)),
            ],
            compiler_params=pltpu.CompilerParams(
                collective_id=0, has_side_effects=True, vmem_limit_bytes=52 * 1024 * 1024
            ),
        )(pos, unnormed, gain.reshape(1, 512), kr, qn, qr, ku, vu, go)
        return out[0], out[1], out[2].reshape(512)

    in_specs = (
        P("dp", "ctx"),
        P("dp", "ctx", None),
        P(),
        P("dp", "ctx", None),
        P("dp", "ctx", "head"),
        P("dp", "ctx", "head"),
        P("head", None, None),
        P("head", None, None),
        P("dp", "ctx", "head"),
    )
    out_specs = (P("dp", ("ctx", "head"), None), P("dp", ("ctx", "head"), None), P())
    return jax.shard_map(
        per_device, mesh=mesh, in_specs=in_specs, out_specs=out_specs, check_vma=False
    )
```

```python
import functools
import math

import jax
import jax.numpy as jnp
from jax import lax
from jax.experimental import pallas as pl
from jax.experimental.pallas import tpu as pltpu
from jax.sharding import PartitionSpec as P

BF16 = jnp.bfloat16
F32 = jnp.float32
MESH = pl.DeviceIdType.MESH


def dot(a, b):
    return jnp.dot(a, b, preferred_element_type=F32)


def dot_t(a, b):
    return lax.dot_general(a, b, (((1,), (1,)), ((), ())), preferred_element_type=F32)


def kernel(
    nz, ny, nx, total_rows,
    pos_in, x_in, gain_in, kr_in, qn_in, qr_in, ku_in, vu_in, go_in,
    raw_ref, rope_ref, gout_ref,
    pos_ref, x_ref, gain_ref, kr_ref, qn_ref, qr_ref, ku_ref, vu_ref, go_ref, sem_in,
    keys, posbuf, qlat, olat, qrp, wbuf, dbuf, diff,
    pown, psib, rsib, zout, zin, yout, yin, yout2, yin2, zout2, zin2, gsend, gx, gy, gc,
    sem_as, sem_ar, sem_ps, sem_pr, sem_ss, sem_sr, sem_zs, sem_zr, sem_ys, sem_yr, sem_gs, sem_gr,
):
    nc = 2 * nz
    half_z = nz // 2
    me = lax.axis_index("ctx")
    y = lax.axis_index("head")
    x = lax.axis_index("dp")
    z = me // 2
    c = lax.rem(me, 2)
    sib = z * 2 + (1 - c)

    def at_z(off):
        return lax.rem(z + off + nz, nz)

    def rem_copy(src, dst, ssem, rsem, dev):
        return pltpu.make_async_remote_copy(
            src_ref=src, dst_ref=dst, send_sem=ssem, recv_sem=rsem, device_id=dev, device_id_type=MESH
        )

    ins = (x_in, kr_in, gain_in, pos_in, qn_in, ku_in, go_in, vu_in, qr_in)
    here = (x_ref, kr_ref, gain_ref, pos_ref, qn_ref, ku_ref, go_ref, vu_ref, qr_ref)
    loads = [pltpu.make_async_copy(a, b, sem_in.at[i]) for i, (a, b) in enumerate(zip(ins, here))]
    for load in loads:
        load.start()

    barrier = pltpu.get_barrier_semaphore()
    for d in range(1, nc):
        pl.semaphore_signal(barrier, inc=1, device_id={"ctx": lax.rem(me + d, nc)}, device_id_type=MESH)
    for d in range(1, ny):
        pl.semaphore_signal(barrier, inc=1, device_id={"head": lax.rem(y + d, ny)}, device_id_type=MESH)
    for d in range(1, nx):
        pl.semaphore_signal(barrier, inc=1, device_id={"dp": lax.rem(x + d, nx)}, device_id_type=MESH)

    for load in loads[0:4]:
        load.wait()
    rows = x_ref[0].astype(F32)
    rms = jnp.sqrt(jnp.mean(rows * rows, axis=-1, keepdims=True) + 1e-06)
    keys[me, 0:128, :] = (rows / rms * gain_ref[...]).astype(BF16)
    ri = lax.broadcasted_iota(jnp.int32, (64, 128), 0)
    ci = lax.broadcasted_iota(jnp.int32, (64, 128), 1)
    rotary = kr_ref[0]
    none = jnp.zeros_like(rotary)
    packed = dot_t((ci == ri).astype(BF16), jnp.concatenate([rotary, none], axis=0)) + dot_t(
        (ci == ri + 64).astype(BF16), jnp.concatenate([none, rotary], axis=0)
    )
    packed = packed.astype(BF16)
    for g in range(4):
        keys[me, 128:144, 128 * g : 128 * g + 128] = packed[16 * g : 16 * g + 16]
    posbuf[me] = pos_ref[...]

    pl.semaphore_wait(barrier, (nc - 1) + (ny - 1) + (nx - 1))

    started = []

    def start(copy):
        copy.start()
        started.append(copy)

    offsets = [0] + [off for t in range(1, half_z) for off in (t, -t)] + [half_z]
    index_of = {off: i for i, off in enumerate(offsets)}
    far = [off for off in offsets if abs(off) > 1]

    def lanes(row):
        return pl.ds(pl.multiple_of(128 * lax.rem(row + ny, 4), 128), 128)

    def z_copy(off, owner):
        i = index_of[off]
        ref = keys.at[owner] if off not in far else keys.at[owner, :, lanes(y)]
        return rem_copy(ref, ref, sem_as.at[0, i], sem_ar.at[0, i], {"ctx": at_z(off) * 2 + c})

    def sib_block(off, core):
        i = index_of[off]
        ref = keys.at[at_z(off) * 2 + core]
        return rem_copy(ref, ref, sem_as.at[1, i], sem_ar.at[1, i], {"ctx": sib})

    def y_quarter(off, way, row):
        i = index_of[off]
        step = (1, -1, 2 - 4 * c)[way]
        ref = keys.at[at_z(off) * 2 + c, :, lanes(row)]
        return rem_copy(
            ref, ref, sem_as.at[2 + way, i], sem_ar.at[2 + way, i], {"head": lax.rem(y + step + ny, ny)}
        )

    def take_far(off):
        z_copy(-off if off != half_z else off, at_z(off) * 2 + c).wait_recv()
        for way in range(3):
            start(y_quarter(off, way, y))

    def take_rest(off):
        if off in far:
            for way in range(3):
                y_quarter(off, way, y - (1, -1, 2)[way]).wait_recv()
        else:
            z_copy(-off if off != half_z else off, at_z(off) * 2 + c).wait_recv()
        start(sib_block(off, c))

    def pos_copy(d, slot):
        return rem_copy(
            posbuf.at[slot], posbuf.at[slot], sem_ps.at[d], sem_pr.at[d], {"ctx": lax.rem(me + d, nc)}
        )

    for d in range(1, nc):
        start(pos_copy(d, me))
    start(sib_block(0, c))
    for off in reversed(offsets[1:]):
        start(z_copy(off, me))

    fi = lax.broadcasted_iota(jnp.int32, (128, 128), 0)
    fj = lax.broadcasted_iota(jnp.int32, (128, 128), 1)
    for load in loads[4:]:
        load.wait()
    for h in range(8):
        part = dot(qn_ref[0, :, 128 * h : 128 * h + 128], ku_ref[h]).astype(BF16)
        qlat[0, 64 * h : 64 * h + 64, :] = part[0:64]
        qlat[1, 64 * h : 64 * h + 64, :] = part[64:128]
        part = dot(go_ref[0, :, 128 * h : 128 * h + 128], vu_ref[h]).astype(BF16)
        olat[0, 64 * h : 64 * h + 64, :] = part[0:64]
        olat[1, 64 * h : 64 * h + 64, :] = part[64:128]
        pair = qr_ref[0, :, 128 * (h // 2) : 128 * (h // 2) + 128]
        e = 64 * (h % 2)
        left = dot(pair, ((fi == fj + e) & (fj < 64)).astype(BF16)).astype(BF16)
        right = dot(pair[64:128], ((fi + 64 - e == fj) & (fj >= 64)).astype(BF16)).astype(BF16)
        qrp[0, 64 * h : 64 * h + 64, :] = left[0:64]
        qrp[1, 64 * h : 64 * h + 64, :] = left[64:128]
        qrp[2, 64 * h : 64 * h + 64, :] = right
    diff[...] = lax.rem(lax.broadcasted_iota(jnp.int32, (64, 512), 1), 64) - lax.broadcasted_iota(
        jnp.int32, (64, 512), 0
    )

    scale = float(128 + 64) ** (-0.5)
    to_log2 = scale * math.log2(math.e)

    groups = [[0]] + [[t, -t] for t in range(1, half_z)] + [[half_z]]
    first = []
    count = 0
    for g in groups:
        first.append(count)
        count += 2 * len(g)

    def blocks_of(g):
        return [at_z(off) * 2 + cc for off in g for cc in range(2)]

    def cat(parts):
        return parts[0] if len(parts) == 1 else jnp.concatenate(parts, axis=0)

    def rope_rows(b):
        return [keys[b, 128:144, 128 * g : 128 * g + 128] for g in range(4)]

    m_up = jnp.full((1, 512), -jnp.inf, F32)
    m_lo = m_up
    l_up = jnp.zeros((1, 512), F32)
    l_lo, d_up, d_lo = l_up, l_up, l_up
    tops = []
    for t, g in enumerate(groups):
        if t == 0:
            for d in range(1, nc):
                pos_copy(d, lax.rem(me - d + nc, nc)).wait_recv()
        else:
            if t == 1:
                for off in far:
                    take_far(off)
            for off in g:
                take_rest(off)
        for off in g:
            sib_block(off, 1 - c).wait_recv()

        blocks = blocks_of(g)
        n = 64 * len(blocks)
        span = pl.ds(64 * first[t], n)
        low = cat([keys[b, 0:64, :] for b in blocks])
        high = cat([keys[b, 64:128, :] for b in blocks])
        rope = cat([r for b in blocks for r in rope_rows(b)])
        wbuf[0, span, :] = (dot_t(low, qlat[1]) + dot_t(rope, qrp[1])) * to_log2
        dbuf[0, span, :] = dot_t(low, olat[1])
        s_high = (dot_t(high, qlat[1]) + dot_t(rope, qrp[2])) * to_log2
        dbuf[1, span, :] = dot_t(high, olat[1])
        s_low = (dot_t(low, qlat[0]) + dot_t(rope, qrp[0])) * to_log2
        dbuf[2, span, :] = dot_t(low, olat[0])
        for i, b in enumerate(blocks):
            sub = pl.ds(64 * (first[t] + i), 64)
            late = posbuf[b, 0:1, 64:65] - pos_ref[0:1, 64:65]
            early = posbuf[b, 0:1, 0:1] - pos_ref[0:1, 0:1]
            wbuf[1, sub, :] = jnp.where(diff[...] >= late, s_high[64 * i : 64 * i + 64], -jnp.inf)
            wbuf[2, sub, :] = jnp.where(diff[...] >= early, s_low[64 * i : 64 * i + 64], -jnp.inf)
        new_up = jnp.maximum(
            m_up,
            jnp.maximum(
                jnp.max(wbuf[0, span, :], axis=0, keepdims=True), jnp.max(wbuf[1, span, :], axis=0, keepdims=True)
            ),
        )
        new_lo = jnp.maximum(m_lo, jnp.max(wbuf[2, span, :], axis=0, keepdims=True))
        a_up = jnp.exp2(m_up - new_up)
        a_lo = jnp.exp2(m_lo - new_lo)
        m_up, m_lo = new_up, new_lo
        l_up, d_up, l_lo, d_lo = l_up * a_up, d_up * a_up, l_lo * a_lo, d_lo * a_lo
        tops.append((m_up, m_lo))
        for kind in range(3):
            top = m_lo if kind == 2 else m_up
            w = jnp.exp2(wbuf[kind, span, :] - top)
            wbuf[kind, span, :] = w
            l_add = jnp.sum(w, axis=0, keepdims=True)
            d_add = jnp.sum(w * dbuf[kind, span, :], axis=0, keepdims=True)
            if kind == 2:
                l_lo, d_lo = l_lo + l_add, d_lo + d_add
            else:
                l_up, d_up = l_up + l_add, d_up + d_add

    inv_up, inv_lo = 1.0 / l_up, 1.0 / l_lo
    delta_up, delta_lo = d_up * inv_up, d_lo * inv_lo

    def sib_copy(index):
        return rem_copy(
            psib.at[index], rsib.at[index], sem_ss.at[index], sem_sr.at[index], {"ctx": sib}
        )

    def z_part(i):
        return rem_copy(
            zout.at[i], zin.at[i], sem_zs.at[0, i], sem_zr.at[0, i], {"ctx": at_z(offsets[i]) * 2 + c}
        )

    cuts = [cut for cut in ([t for t in range(3, half_z + 1)], [2], [0, 1]) if cut and cut[0] <= half_z]

    def y_part(k, d):
        begin = index_of[groups[cuts[k][0]][0]]
        size = sum(len(groups[t]) for t in cuts[k])
        peer = lax.rem(y + d, ny)
        return rem_copy(
            yout.at[peer, pl.ds(begin, size)], yin.at[d - 1, pl.ds(begin, size)],
            sem_ys.at[k, d], sem_yr.at[k, d], {"head": peer},
        )

    def send_on(t):
        for off in groups[t]:
            i = index_of[off]
            sib_copy(i).wait_recv()
            total = (pown[i].astype(F32) + rsib[i].astype(F32)).astype(BF16)
            zout[i] = total[0:160]
            if off != 0:
                start(z_part(i))
            for k in range(ny):
                yout[k, i] = total[160 + 16 * k : 176 + 16 * k]
        for k, cut in enumerate(cuts):
            if cut[0] == t:
                for d in range(1, ny):
                    start(y_part(k, d))

    gain_acc = jnp.zeros((1, 512), F32)
    for t in reversed(range(len(groups))):
        g = groups[t]
        blocks = blocks_of(g)
        n = 64 * len(blocks)
        span = pl.ds(64 * first[t], n)
        c_up = jnp.exp2(tops[t][0] - m_up) * inv_up
        c_lo = jnp.exp2(tops[t][1] - m_lo) * inv_lo
        probs = []
        dscores = []
        for kind in range(3):
            factor, delta = (c_lo, delta_lo) if kind == 2 else (c_up, delta_up)
            p = wbuf[kind, span, :] * factor
            probs.append(p.astype(BF16))
            dscores.append((p * (dbuf[kind, span, :] - delta) * scale).astype(BF16))
        lat_low = (
            dot(probs[0], olat[1]) + dot(dscores[0], qlat[1]) + dot(probs[2], olat[0]) + dot(dscores[2], qlat[0])
        )
        lat_high = dot(probs[1], olat[1]) + dot(dscores[1], qlat[1])
        rope = dot(dscores[0], qrp[1]) + dot(dscores[1], qrp[2]) + dot(dscores[2], qrp[0])
        low = cat([keys[b, 0:64, :] for b in blocks])
        high = cat([keys[b, 64:128, :] for b in blocks])
        gain_acc = gain_acc + jnp.sum(
            lat_low * low.astype(F32) + lat_high * high.astype(F32), axis=0, keepdims=True
        )
        lat_low = lat_low.astype(BF16)
        lat_high = lat_high.astype(BF16)
        rope = rope.astype(BF16)
        for i, b in enumerate(blocks):
            index = index_of[g[i // 2]]

            def put(buf):
                buf[index, 0:64, :] = lat_low[64 * i : 64 * i + 64, 0:256]
                buf[index, 64:128, :] = lat_high[64 * i : 64 * i + 64, 0:256]
                for k in range(4):
                    buf[index, 128 + 16 * (k // 2) : 144 + 16 * (k // 2), 128 * (k % 2) : 128 * (k % 2) + 128] = rope[
                        64 * i + 16 * k : 64 * i + 16 * k + 16
                    ]
                buf[index, 160:224, :] = lat_low[64 * i : 64 * i + 64, 256:512]
                buf[index, 224:288, :] = lat_high[64 * i : 64 * i + 64, 256:512]

            @pl.when(c == i % 2)
            def _():
                put(pown)

            @pl.when(c != i % 2)
            def _():
                put(psib)

        for off in g:
            start(sib_copy(index_of[off]))
        if t < half_z:
            send_on(t + 1)

    gsend[0] = gain_acc

    def gain_copy(stage, d, slot):
        buf, base, axis, pos, size = (
            (gx, 0, "dp", x, nx), (gy, nx - 1, "head", y, ny), (gc, nx + ny - 2, "ctx", me, nc)
        )[stage]
        return rem_copy(
            gsend.at[stage], buf.at[slot], sem_gs.at[base + d - 1], sem_gr.at[base + d - 1],
            {axis: lax.rem(pos + d, size)},
        )

    def gain_send(stage):
        buf, pos, size = ((gx, x, nx), (gy, y, ny), (gc, me, nc))[stage]
        buf[pos] = gsend[stage]
        for d in range(1, size):
            start(gain_copy(stage, d, pos))

    def gain_sum(stage):
        buf, pos, size = ((gx, x, nx), (gy, y, ny), (gc, me, nc))[stage]
        for d in range(1, size):
            gain_copy(stage, d, lax.rem(pos - d + size, size)).wait_recv()
        return jnp.sum(buf[...], axis=0)

    gain_send(0)
    send_on(0)
    gsend[1] = gain_sum(0)
    gain_send(1)

    total = zout[0].astype(F32)
    for i in range(1, nz):
        z_part(i).wait_recv()
        total = total + zin[i].astype(F32)
    total = total.astype(BF16)
    for k in range(ny):
        q = k % 4
        yout2[k, :, 0:256] = total[16 * k : 16 * k + 16]
        yout2[k, :, 256:384] = total[128 + 16 * (q // 2) : 144 + 16 * (q // 2), 128 * (q % 2) : 128 * (q % 2) + 128]

    def y_last(d):
        peer = lax.rem(y + d, ny)
        return rem_copy(yout2.at[peer], yin2.at[d], sem_ys.at[3, d], sem_yr.at[3, d], {"head": peer})

    for d in range(1, ny):
        start(y_last(d))
    gsend[2] = gain_sum(1)
    gain_send(2)

    def z_last(i):
        return rem_copy(
            zout2.at[i], zin2.at[i], sem_zs.at[1, i], sem_zr.at[1, i], {"ctx": at_z(offsets[i]) * 2 + c}
        )

    for k in range(len(cuts)):
        for d in range(1, ny):
            y_part(k, d).wait_recv()
    right = yout[y].astype(F32)
    for d in range(1, ny):
        right = right + yin[d - 1].astype(F32)
    zout2[...] = right.astype(BF16)
    for i in range(1, nz):
        start(z_last(i))

    left = yout2[y].astype(F32)
    for d in range(1, ny):
        y_last(d).wait_recv()
        left = left + yin2[d].astype(F32)
    right = zout2[0].astype(F32)
    for i in range(1, nz):
        z_last(i).wait_recv()
        right = right + zin2[i].astype(F32)

    cot = jnp.concatenate([left[:, 0:256], right], axis=1)
    own = x_ref[0, pl.ds(pl.multiple_of(16 * y, 16), 16), :].astype(F32)
    own_rms = jnp.sqrt(jnp.mean(own * own, axis=-1, keepdims=True) + 1e-06)
    xhat = own / own_rms
    scaled = gain_ref[...] * cot
    raw_ref[0] = (scaled - xhat * jnp.mean(scaled * xhat, axis=-1, keepdims=True)) / own_rms
    both = left[:, 256:384]
    rope_ref[0] = jnp.where(y >= ny // 2, pltpu.roll(both, 64, 1), both)[:, 0:64]

    gout_ref[...] = gain_sum(2) / gain_ref[...] * (1.0 / math.sqrt(total_rows))
    for copy in started:
        copy.wait_send()


def solution(mesh):
    nc, ny, nx = mesh.shape["ctx"], mesh.shape["head"], mesh.shape["dp"]
    nz = nc // 2
    half_z = nz // 2

    def per_device(pos, unnormed, gain, kr, qn, qr, ku, vu, go):
        dma = pltpu.SemaphoreType.DMA
        out = pl.pallas_call(
            functools.partial(kernel, nz, ny, nx, nc * 128 * nx),
            out_shape=(
                jax.ShapeDtypeStruct((1, 16, 512), F32),
                jax.ShapeDtypeStruct((1, 16, 64), F32),
                jax.ShapeDtypeStruct((1, 512), F32),
            ),
            in_specs=[pl.BlockSpec(memory_space=pl.ANY)] * 9,
            out_specs=[pl.BlockSpec(memory_space=pltpu.VMEM)] * 3,
            scratch_shapes=[
                pltpu.VMEM((1, 128), jnp.int32),
                pltpu.VMEM((1, 128, 512), BF16),
                pltpu.VMEM((1, 512), F32),
                pltpu.VMEM((1, 64, 128), BF16),
                pltpu.VMEM((1, 128, 1024), BF16),
                pltpu.VMEM((1, 128, 512), BF16),
                pltpu.VMEM((8, 128, 512), BF16),
                pltpu.VMEM((8, 128, 512), BF16),
                pltpu.VMEM((1, 128, 1024), BF16),
                dma((9,)),
                pltpu.VMEM((nc, 144, 512), BF16),
                pltpu.VMEM((nc, 1, 128), jnp.int32),
                pltpu.VMEM((2, 512, 512), BF16),
                pltpu.VMEM((2, 512, 512), BF16),
                pltpu.VMEM((3, 512, 128), BF16),
                pltpu.VMEM((3, 64 * nc, 512), F32),
                pltpu.VMEM((3, 64 * nc, 512), F32),
                pltpu.VMEM((64, 512), jnp.int32),
                pltpu.VMEM((nz, 288, 256), BF16),
                pltpu.VMEM((nz, 288, 256), BF16),
                pltpu.VMEM((nz, 288, 256), BF16),
                pltpu.VMEM((nz, 160, 256), BF16),
                pltpu.VMEM((nz, 160, 256), BF16),
                pltpu.VMEM((ny, nz, 16, 256), BF16),
                pltpu.VMEM((ny, nz, 16, 256), BF16),
                pltpu.VMEM((ny, 16, 384), BF16),
                pltpu.VMEM((ny, 16, 384), BF16),
                pltpu.VMEM((nz, 16, 256), BF16),
                pltpu.VMEM((nz, 16, 256), BF16),
                pltpu.VMEM((3, 1, 512), F32),
                pltpu.VMEM((nx, 1, 512), F32),
                pltpu.VMEM((ny, 1, 512), F32),
                pltpu.VMEM((nc, 1, 512), F32),
                dma((5, nz)),
                dma((5, nz)),
                dma((nc,)),
                dma((nc,)),
                dma((nz,)),
                dma((nz,)),
                dma((2, nz)),
                dma((2, nz)),
                dma((4, ny)),
                dma((4, ny)),
                dma((nx + ny + nc,)),
                dma((nx + ny + nc,)),
            ],
            compiler_params=pltpu.CompilerParams(
                collective_id=0, has_side_effects=True, vmem_limit_bytes=60 * 1024 * 1024
            ),
        )(pos, unnormed, gain.reshape(1, 512), jnp.swapaxes(kr, 1, 2), qn, qr, ku, vu, go)
        return out[0], out[1], out[2].reshape(512)

    in_specs = (
        P("dp", "ctx"),
        P("dp", "ctx", None),
        P(),
        P("dp", "ctx", None),
        P("dp", "ctx", "head"),
        P("dp", "ctx", "head"),
        P("head", None, None),
        P("head", None, None),
        P("dp", "ctx", "head"),
    )
    out_specs = (P("dp", ("ctx", "head"), None), P("dp", ("ctx", "head"), None), P())
    return jax.shard_map(
        per_device, mesh=mesh, in_specs=in_specs, out_specs=out_specs, check_vma=False
    )
```

```python
import functools
import math

import jax
import jax.numpy as jnp
from jax import lax
from jax.experimental import pallas as pl
from jax.experimental.pallas import tpu as pltpu
from jax.sharding import PartitionSpec as P

BF16 = jnp.bfloat16
F32 = jnp.float32
MESH = pl.DeviceIdType.MESH


def dot(a, b):
    return jnp.dot(a, b, preferred_element_type=F32)


def dot_t(a, b):
    return lax.dot_general(a, b, (((1,), (1,)), ((), ())), preferred_element_type=F32)


def kernel(
    nz, ny, nx, total_rows,
    pos_in, x_in, gain_in, kr_in, qn_in, qr_in, ku_in, vu_in, go_in,
    raw_ref, rope_ref, gout_ref,
    pos_ref, x_ref, gain_ref, kr_ref, qn_ref, qr_ref, ku_ref, vu_ref, go_ref, sem_in,
    keys, posbuf, qlat, olat, qrp, wbuf, dbuf, diff,
    pown, psib, rsib, zout, zin, yout, yin, yout2, yin2, zout2, zin2, gsend, gx, gy, gc,
    sem_as, sem_ar, sem_ps, sem_pr, sem_ss, sem_sr, sem_zs, sem_zr, sem_ys, sem_yr, sem_gs, sem_gr,
):
    nc = 2 * nz
    half_z = nz // 2
    me = lax.axis_index("ctx")
    y = lax.axis_index("head")
    x = lax.axis_index("dp")
    z = me // 2
    c = lax.rem(me, 2)
    sib = z * 2 + (1 - c)

    def at_z(off):
        return lax.rem(z + off + nz, nz)

    def rem_copy(src, dst, ssem, rsem, dev):
        return pltpu.make_async_remote_copy(
            src_ref=src, dst_ref=dst, send_sem=ssem, recv_sem=rsem, device_id=dev, device_id_type=MESH
        )

    ins = (x_in, kr_in, gain_in, pos_in, qn_in, ku_in, go_in, vu_in, qr_in)
    here = (x_ref, kr_ref, gain_ref, pos_ref, qn_ref, ku_ref, go_ref, vu_ref, qr_ref)
    loads = [pltpu.make_async_copy(a, b, sem_in.at[i]) for i, (a, b) in enumerate(zip(ins, here))]
    for load in loads[0:4]:
        load.start()

    barrier = pltpu.get_barrier_semaphore()
    for d in range(1, nc):
        pl.semaphore_signal(barrier, inc=1, device_id={"ctx": lax.rem(me + d, nc)}, device_id_type=MESH)
    for d in range(1, ny):
        pl.semaphore_signal(barrier, inc=1, device_id={"head": lax.rem(y + d, ny)}, device_id_type=MESH)
    for d in range(1, nx):
        pl.semaphore_signal(barrier, inc=1, device_id={"dp": lax.rem(x + d, nx)}, device_id_type=MESH)

    for load in loads[4:]:
        load.start()

    for load in loads[0:4]:
        load.wait()
    rows = x_ref[0].astype(F32)
    rms = jnp.sqrt(jnp.mean(rows * rows, axis=-1, keepdims=True) + 1e-06)
    keys[me, 0:128, :] = (rows / rms * gain_ref[...]).astype(BF16)
    ri = lax.broadcasted_iota(jnp.int32, (64, 128), 0)
    ci = lax.broadcasted_iota(jnp.int32, (64, 128), 1)
    rotary = kr_ref[0]
    none = jnp.zeros_like(rotary)
    packed = dot_t((ci == ri).astype(BF16), jnp.concatenate([rotary, none], axis=0)) + dot_t(
        (ci == ri + 64).astype(BF16), jnp.concatenate([none, rotary], axis=0)
    )
    packed = packed.astype(BF16)
    for g in range(4):
        keys[me, 128:144, 128 * g : 128 * g + 128] = packed[16 * g : 16 * g + 16]
    posbuf[me] = pos_ref[...]

    pl.semaphore_wait(barrier, (nc - 1) + (ny - 1) + (nx - 1))

    started = []

    def start(copy):
        copy.start()
        started.append(copy)

    offsets = [0] + [off for t in range(1, half_z) for off in (t, -t)] + [half_z]
    index_of = {off: i for i, off in enumerate(offsets)}
    far = [off for off in offsets if abs(off) > 1]

    def lanes(row):
        return pl.ds(pl.multiple_of(128 * lax.rem(row + ny, 4), 128), 128)

    def z_copy(off, owner):
        i = index_of[off]
        ref = keys.at[owner] if off not in far else keys.at[owner, :, lanes(y)]
        return rem_copy(ref, ref, sem_as.at[0, i], sem_ar.at[0, i], {"ctx": at_z(off) * 2 + c})

    def sib_block(off, core):
        i = index_of[off]
        ref = keys.at[at_z(off) * 2 + core]
        return rem_copy(ref, ref, sem_as.at[1, i], sem_ar.at[1, i], {"ctx": sib})

    def y_quarter(off, way, row):
        i = index_of[off]
        step = (1, -1, 2 - 4 * c)[way]
        ref = keys.at[at_z(off) * 2 + c, :, lanes(row)]
        return rem_copy(
            ref, ref, sem_as.at[2 + way, i], sem_ar.at[2 + way, i], {"head": lax.rem(y + step + ny, ny)}
        )

    def take_far(off):
        z_copy(-off if off != half_z else off, at_z(off) * 2 + c).wait_recv()
        for way in range(3):
            start(y_quarter(off, way, y))

    def take_rest(off):
        if off in far:
            for way in range(3):
                y_quarter(off, way, y - (1, -1, 2)[way]).wait_recv()
        else:
            z_copy(-off if off != half_z else off, at_z(off) * 2 + c).wait_recv()
        start(sib_block(off, c))

    def pos_copy(d, slot):
        return rem_copy(
            posbuf.at[slot], posbuf.at[slot], sem_ps.at[d], sem_pr.at[d], {"ctx": lax.rem(me + d, nc)}
        )

    for off in far:
        start(z_copy(off, me))
    start(sib_block(0, c))
    for d in range(1, nc):
        start(pos_copy(d, me))
    for off in offsets[1:3]:
        start(z_copy(off, me))

    fi = lax.broadcasted_iota(jnp.int32, (128, 128), 0)
    fj = lax.broadcasted_iota(jnp.int32, (128, 128), 1)
    for load in loads[4:]:
        load.wait()
    for h in range(8):
        part = dot(qn_ref[0, :, 128 * h : 128 * h + 128], ku_ref[h]).astype(BF16)
        qlat[0, 64 * h : 64 * h + 64, :] = part[0:64]
        qlat[1, 64 * h : 64 * h + 64, :] = part[64:128]
        part = dot(go_ref[0, :, 128 * h : 128 * h + 128], vu_ref[h]).astype(BF16)
        olat[0, 64 * h : 64 * h + 64, :] = part[0:64]
        olat[1, 64 * h : 64 * h + 64, :] = part[64:128]
        pair = qr_ref[0, :, 128 * (h // 2) : 128 * (h // 2) + 128]
        e = 64 * (h % 2)
        left = dot(pair, ((fi == fj + e) & (fj < 64)).astype(BF16)).astype(BF16)
        right = dot(pair[64:128], ((fi + 64 - e == fj) & (fj >= 64)).astype(BF16)).astype(BF16)
        qrp[0, 64 * h : 64 * h + 64, :] = left[0:64]
        qrp[1, 64 * h : 64 * h + 64, :] = left[64:128]
        qrp[2, 64 * h : 64 * h + 64, :] = right
    diff[...] = lax.rem(lax.broadcasted_iota(jnp.int32, (64, 512), 1), 64) - lax.broadcasted_iota(
        jnp.int32, (64, 512), 0
    )

    scale = float(128 + 64) ** (-0.5)
    to_log2 = scale * math.log2(math.e)

    groups = [[0]] + [[t, -t] for t in range(1, half_z)] + [[half_z]]
    first = []
    count = 0
    for g in groups:
        first.append(count)
        count += 2 * len(g)

    def blocks_of(g):
        return [at_z(off) * 2 + cc for off in g for cc in range(2)]

    def cat(parts):
        return parts[0] if len(parts) == 1 else jnp.concatenate(parts, axis=0)

    def rope_rows(b):
        return [keys[b, 128:144, 128 * g : 128 * g + 128] for g in range(4)]

    m_up = jnp.full((1, 512), -jnp.inf, F32)
    m_lo = m_up
    l_up = jnp.zeros((1, 512), F32)
    l_lo, d_up, d_lo = l_up, l_up, l_up
    tops = []
    for t, g in enumerate(groups):
        if t == 0:
            for off in far:
                take_far(off)
            for d in range(1, nc):
                pos_copy(d, lax.rem(me - d + nc, nc)).wait_recv()
        else:
            if t < half_z:
                for off in g + (groups[t + 1] if t + 1 == half_z else []):
                    take_rest(off)
        for off in g:
            sib_block(off, 1 - c).wait_recv()

        blocks = blocks_of(g)
        n = 64 * len(blocks)
        span = pl.ds(64 * first[t], n)
        low = cat([keys[b, 0:64, :] for b in blocks])
        high = cat([keys[b, 64:128, :] for b in blocks])
        rope = cat([r for b in blocks for r in rope_rows(b)])
        wbuf[0, span, :] = (dot_t(low, qlat[1]) + dot_t(rope, qrp[1])) * to_log2
        dbuf[0, span, :] = dot_t(low, olat[1])
        s_high = (dot_t(high, qlat[1]) + dot_t(rope, qrp[2])) * to_log2
        dbuf[1, span, :] = dot_t(high, olat[1])
        s_low = (dot_t(low, qlat[0]) + dot_t(rope, qrp[0])) * to_log2
        dbuf[2, span, :] = dot_t(low, olat[0])
        for i, b in enumerate(blocks):
            sub = pl.ds(64 * (first[t] + i), 64)
            late = posbuf[b, 0:1, 64:65] - pos_ref[0:1, 64:65]
            early = posbuf[b, 0:1, 0:1] - pos_ref[0:1, 0:1]
            wbuf[1, sub, :] = jnp.where(diff[...] >= late, s_high[64 * i : 64 * i + 64], -jnp.inf)
            wbuf[2, sub, :] = jnp.where(diff[...] >= early, s_low[64 * i : 64 * i + 64], -jnp.inf)
        new_up = jnp.maximum(
            m_up,
            jnp.maximum(
                jnp.max(wbuf[0, span, :], axis=0, keepdims=True), jnp.max(wbuf[1, span, :], axis=0, keepdims=True)
            ),
        )
        new_lo = jnp.maximum(m_lo, jnp.max(wbuf[2, span, :], axis=0, keepdims=True))
        a_up = jnp.exp2(m_up - new_up)
        a_lo = jnp.exp2(m_lo - new_lo)
        m_up, m_lo = new_up, new_lo
        l_up, d_up, l_lo, d_lo = l_up * a_up, d_up * a_up, l_lo * a_lo, d_lo * a_lo
        tops.append((m_up, m_lo))
        for kind in range(3):
            top = m_lo if kind == 2 else m_up
            w = jnp.exp2(wbuf[kind, span, :] - top)
            wbuf[kind, span, :] = w
            l_add = jnp.sum(w, axis=0, keepdims=True)
            d_add = jnp.sum(w * dbuf[kind, span, :], axis=0, keepdims=True)
            if kind == 2:
                l_lo, d_lo = l_lo + l_add, d_lo + d_add
            else:
                l_up, d_up = l_up + l_add, d_up + d_add

    inv_up, inv_lo = 1.0 / l_up, 1.0 / l_lo
    delta_up, delta_lo = d_up * inv_up, d_lo * inv_lo

    def sib_copy(index):
        return rem_copy(
            psib.at[index], rsib.at[index], sem_ss.at[index], sem_sr.at[index], {"ctx": sib}
        )

    relayed = half_z == 4
    stops = {3: 1, -3: -1, 4: 2 - 4 * c} if relayed else {}

    def z_part(i):
        off = offsets[i]
        return rem_copy(
            zout.at[i], zin.at[i], sem_zs.at[0, i], sem_zr.at[0, i], {"ctx": at_z(stops.get(off, off)) * 2 + c}
        )

    def relay():
        for off in (3, -3, 4):
            z_part(index_of[off]).wait_recv()
        for off, source, core in ((2, 3, 0), (-2, -3, 1)):
            i = index_of[off]
            total = pown[i, 0:160].astype(F32) + rsib[i, 0:160].astype(F32) + zin[index_of[source]].astype(F32)
            zout[i] = (total + jnp.where(c == core, zin[index_of[4]].astype(F32), 0.0)).astype(BF16)
            start(z_part(i))

    cuts = [[t] for t in range(half_z, -1, -1)]

    def y_part(k, d):
        begin = index_of[groups[cuts[k][0]][0]]
        size = sum(len(groups[t]) for t in cuts[k])
        peer = lax.rem(y + d, ny)
        stop = lax.rem(y + {3: 1, 5: 7, 4: 2 + 4 * c}.get(d, d), ny) if y_relayed(k) else peer
        return rem_copy(
            yout.at[peer, pl.ds(begin, size)], yin.at[d - 1, pl.ds(begin, size)],
            sem_ys.at[k, d], sem_yr.at[k, d], {"head": stop},
        )

    def y_relayed(k):
        return ny == 8 and cuts[k][0] > 1

    def y_relay(k):
        begin = index_of[groups[cuts[k][0]][0]]
        span = pl.ds(begin, sum(len(groups[t]) for t in cuts[k]))
        for d in (3, 5, 4):
            y_part(k, d).wait_recv()
        for d, source, core in ((2, 3, 0), (6, 5, 1)):
            peer = lax.rem(y + d, ny)
            total = yout[peer, span].astype(F32) + yin[source - 1, span].astype(F32)
            yout[peer, span] = (total + jnp.where(c == core, yin[3, span].astype(F32), 0.0)).astype(BF16)
            start(y_part(k, d))

    def send_on(t):
        for off in groups[t]:
            i = index_of[off]
            sib_copy(i).wait_recv()
            total = (pown[i].astype(F32) + rsib[i].astype(F32)).astype(BF16)
            if not relayed or abs(off) != 2:
                zout[i] = total[0:160]
                if off != 0:
                    start(z_part(i))
            for k in range(ny):
                yout[k, i] = total[160 + 16 * k : 176 + 16 * k]
        for k, cut in enumerate(cuts):
            if cut[0] == t:
                for d in range(1, ny):
                    if not (y_relayed(k) and d in (2, 6)):
                        start(y_part(k, d))

    gain_acc = jnp.zeros((1, 512), F32)
    for t in reversed(range(len(groups))):
        g = groups[t]
        blocks = blocks_of(g)
        n = 64 * len(blocks)
        span = pl.ds(64 * first[t], n)
        c_up = jnp.exp2(tops[t][0] - m_up) * inv_up
        c_lo = jnp.exp2(tops[t][1] - m_lo) * inv_lo
        probs = []
        dscores = []
        for kind in range(3):
            factor, delta = (c_lo, delta_lo) if kind == 2 else (c_up, delta_up)
            p = wbuf[kind, span, :] * factor
            probs.append(p.astype(BF16))
            dscores.append((p * (dbuf[kind, span, :] - delta) * scale).astype(BF16))
        lat_low = (
            dot(probs[0], olat[1]) + dot(dscores[0], qlat[1]) + dot(probs[2], olat[0]) + dot(dscores[2], qlat[0])
        )
        lat_high = dot(probs[1], olat[1]) + dot(dscores[1], qlat[1])
        rope = dot(dscores[0], qrp[1]) + dot(dscores[1], qrp[2]) + dot(dscores[2], qrp[0])
        low = cat([keys[b, 0:64, :] for b in blocks])
        high = cat([keys[b, 64:128, :] for b in blocks])
        gain_acc = gain_acc + jnp.sum(
            lat_low * low.astype(F32) + lat_high * high.astype(F32), axis=0, keepdims=True
        )
        lat_low = lat_low.astype(BF16)
        lat_high = lat_high.astype(BF16)
        rope = rope.astype(BF16)
        for i, b in enumerate(blocks):
            index = index_of[g[i // 2]]

            def put(buf):
                buf[index, 0:64, :] = lat_low[64 * i : 64 * i + 64, 0:256]
                buf[index, 64:128, :] = lat_high[64 * i : 64 * i + 64, 0:256]
                for k in range(4):
                    buf[index, 128 + 16 * (k // 2) : 144 + 16 * (k // 2), 128 * (k % 2) : 128 * (k % 2) + 128] = rope[
                        64 * i + 16 * k : 64 * i + 16 * k + 16
                    ]
                buf[index, 160:224, :] = lat_low[64 * i : 64 * i + 64, 256:512]
                buf[index, 224:288, :] = lat_high[64 * i : 64 * i + 64, 256:512]

            @pl.when(c == i % 2)
            def _():
                put(pown)

            @pl.when(c != i % 2)
            def _():
                put(psib)

        for off in g:
            start(sib_copy(index_of[off]))
        if t < half_z:
            send_on(t + 1)

    gsend[0] = gain_acc

    def gain_copy(stage, d, slot):
        buf, base, axis, pos, size = (
            (gx, 0, "dp", x, nx), (gy, nx - 1, "head", y, ny), (gc, nx + ny - 2, "ctx", me, nc)
        )[stage]
        return rem_copy(
            gsend.at[stage], buf.at[slot], sem_gs.at[base + d - 1], sem_gr.at[base + d - 1],
            {axis: lax.rem(pos + d, size)},
        )

    def gain_send(stage):
        buf, pos, size = ((gx, x, nx), (gy, y, ny), (gc, me, nc))[stage]
        buf[pos] = gsend[stage]
        for d in range(1, size):
            start(gain_copy(stage, d, pos))

    def gain_sum(stage):
        buf, pos, size = ((gx, x, nx), (gy, y, ny), (gc, me, nc))[stage]
        for d in range(1, size):
            gain_copy(stage, d, lax.rem(pos - d + size, size)).wait_recv()
        return jnp.sum(buf[...], axis=0)

    gain_send(0)
    send_on(0)
    if y_relayed(0):
        y_relay(0)
    if relayed:
        relay()
    for k in range(1, len(cuts)):
        if y_relayed(k):
            y_relay(k)
    gsend[1] = gain_sum(0)
    gain_send(1)

    total = zout[0].astype(F32)
    for i in range(1, nz):
        if offsets[i] not in stops:
            z_part(i).wait_recv()
            total = total + zin[i].astype(F32)
    total = total.astype(BF16)
    for k in range(ny):
        q = k % 4
        yout2[k, :, 0:256] = total[16 * k : 16 * k + 16]
        yout2[k, :, 256:384] = total[128 + 16 * (q // 2) : 144 + 16 * (q // 2), 128 * (q % 2) : 128 * (q % 2) + 128]

    def y_last(d):
        peer = lax.rem(y + d, ny)
        return rem_copy(yout2.at[peer], yin2.at[d], sem_ys.at[half_z + 1, d], sem_yr.at[half_z + 1, d], {"head": peer})

    for d in range(1, ny):
        start(y_last(d))
    gsend[2] = gain_sum(1)
    gain_send(2)

    def z_last(i):
        return rem_copy(
            zout2.at[i], zin2.at[i], sem_zs.at[1, i], sem_zr.at[1, i], {"ctx": at_z(offsets[i]) * 2 + c}
        )

    for k, cut in enumerate(cuts):
        begin = index_of[groups[cut[0]][0]]
        span = pl.ds(begin, sum(len(groups[t]) for t in cut))
        right = yout[y, span].astype(F32)
        for d in range(1, ny):
            if not (y_relayed(k) and d in (3, 4, 5)):
                y_part(k, d).wait_recv()
                right = right + yin[d - 1, span].astype(F32)
        zout2[span] = right.astype(BF16)
    for i in range(1, nz):
        start(z_last(i))

    left = yout2[y].astype(F32)
    for d in range(1, ny):
        y_last(d).wait_recv()
        left = left + yin2[d].astype(F32)
    right = zout2[0].astype(F32)
    for i in range(1, nz):
        z_last(i).wait_recv()
        right = right + zin2[i].astype(F32)

    cot = jnp.concatenate([left[:, 0:256], right], axis=1)
    own = x_ref[0, pl.ds(pl.multiple_of(16 * y, 16), 16), :].astype(F32)
    own_rms = jnp.sqrt(jnp.mean(own * own, axis=-1, keepdims=True) + 1e-06)
    xhat = own / own_rms
    scaled = gain_ref[...] * cot
    raw_ref[0] = (scaled - xhat * jnp.mean(scaled * xhat, axis=-1, keepdims=True)) / own_rms
    both = left[:, 256:384]
    rope_ref[0] = jnp.where(y >= ny // 2, pltpu.roll(both, 64, 1), both)[:, 0:64]

    gout_ref[...] = gain_sum(2) / gain_ref[...] * (1.0 / math.sqrt(total_rows))
    for copy in started:
        copy.wait_send()


def hand_over(raw_in, rope_in, gain_in, raw_out, rope_out, gain_out):
    raw_out[...] = raw_in[...]
    rope_out[...] = rope_in[...]
    gain_out[...] = gain_in[...]


def solution(mesh):
    nc, ny, nx = mesh.shape["ctx"], mesh.shape["head"], mesh.shape["dp"]
    nz = nc // 2
    half_z = nz // 2

    def per_device(pos, unnormed, gain, kr, qn, qr, ku, vu, go):
        dma = pltpu.SemaphoreType.DMA
        out = pl.pallas_call(
            functools.partial(kernel, nz, ny, nx, nc * 128 * nx),
            out_shape=(
                jax.ShapeDtypeStruct((1, 16, 512), F32),
                jax.ShapeDtypeStruct((1, 16, 64), F32),
                jax.ShapeDtypeStruct((1, 512), F32),
            ),
            in_specs=[pl.BlockSpec(memory_space=pltpu.HBM)] * 9,
            out_specs=[pl.BlockSpec(memory_space=pltpu.VMEM)] * 3,
            scratch_shapes=[
                pltpu.VMEM((1, 128), jnp.int32),
                pltpu.VMEM((1, 128, 512), BF16),
                pltpu.VMEM((1, 512), F32),
                pltpu.VMEM((1, 64, 128), BF16),
                pltpu.VMEM((1, 128, 1024), BF16),
                pltpu.VMEM((1, 128, 512), BF16),
                pltpu.VMEM((8, 128, 512), BF16),
                pltpu.VMEM((8, 128, 512), BF16),
                pltpu.VMEM((1, 128, 1024), BF16),
                dma((9,)),
                pltpu.VMEM((nc, 144, 512), BF16),
                pltpu.VMEM((nc, 1, 128), jnp.int32),
                pltpu.VMEM((2, 512, 512), BF16),
                pltpu.VMEM((2, 512, 512), BF16),
                pltpu.VMEM((3, 512, 128), BF16),
                pltpu.VMEM((3, 64 * nc, 512), F32),
                pltpu.VMEM((3, 64 * nc, 512), F32),
                pltpu.VMEM((64, 512), jnp.int32),
                pltpu.VMEM((nz, 288, 256), BF16),
                pltpu.VMEM((nz, 288, 256), BF16),
                pltpu.VMEM((nz, 288, 256), BF16),
                pltpu.VMEM((nz, 160, 256), BF16),
                pltpu.VMEM((nz, 160, 256), BF16),
                pltpu.VMEM((ny, nz, 16, 256), BF16),
                pltpu.VMEM((ny, nz, 16, 256), BF16),
                pltpu.VMEM((ny, 16, 384), BF16),
                pltpu.VMEM((ny, 16, 384), BF16),
                pltpu.VMEM((nz, 16, 256), BF16),
                pltpu.VMEM((nz, 16, 256), BF16),
                pltpu.VMEM((3, 1, 512), F32),
                pltpu.VMEM((nx, 1, 512), F32),
                pltpu.VMEM((ny, 1, 512), F32),
                pltpu.VMEM((nc, 1, 512), F32),
                dma((5, nz)),
                dma((5, nz)),
                dma((nc,)),
                dma((nc,)),
                dma((nz,)),
                dma((nz,)),
                dma((2, nz)),
                dma((2, nz)),
                dma((half_z + 2, ny)),
                dma((half_z + 2, ny)),
                dma((nx + ny + nc,)),
                dma((nx + ny + nc,)),
            ],
            compiler_params=pltpu.CompilerParams(
                collective_id=0, has_side_effects=True, vmem_limit_bytes=60 * 1024 * 1024
            ),
        )(pos, unnormed, gain.reshape(1, 512), jnp.swapaxes(kr, 1, 2), qn, qr, ku, vu, go)
        out = pl.pallas_call(
            hand_over,
            out_shape=tuple(jax.ShapeDtypeStruct(o.shape, F32) for o in out),
            in_specs=[pl.BlockSpec(memory_space=pltpu.VMEM)] * 3,
            out_specs=[pl.BlockSpec(memory_space=pltpu.VMEM)] * 3,
        )(*out)
        return out[0], out[1], out[2].reshape(512)

    in_specs = (
        P("dp", "ctx"),
        P("dp", "ctx", None),
        P(),
        P("dp", "ctx", None),
        P("dp", "ctx", "head"),
        P("dp", "ctx", "head"),
        P("head", None, None),
        P("head", None, None),
        P("dp", "ctx", "head"),
    )
    out_specs = (P("dp", ("ctx", "head"), None), P("dp", ("ctx", "head"), None), P())
    return jax.shard_map(
        per_device, mesh=mesh, in_specs=in_specs, out_specs=out_specs, check_vma=False
    )
```

```python
import functools
import math

import jax
import jax.numpy as jnp
from jax import lax
from jax.experimental import pallas as pl
from jax.experimental.pallas import tpu as pltpu
from jax.sharding import PartitionSpec as P

BF16 = jnp.bfloat16
F32 = jnp.float32
MESH = pl.DeviceIdType.MESH


def dot(a, b):
    return jnp.dot(a, b, preferred_element_type=F32)


def dot_t(a, b):
    return lax.dot_general(a, b, (((1,), (1,)), ((), ())), preferred_element_type=F32)


def kernel(
    nz, ny, nx, total_rows,
    pos_in, x_in, gain_in, kr_in, qn_in, qr_in, ku_in, vu_in, go_in,
    raw_ref, rope_ref, gout_ref,
    pos_ref, x_ref, gain_ref, kr_ref, qn_ref, qr_ref, ku_ref, vu_ref, go_ref, sem_in,
    keys, posbuf, qlat, olat, qrp, wbuf, dbuf, diff,
    pown, psib, rsib, zout, zin, yout, yin, yout2, yin2, zout2, zin2, gsend, gx, gy, gc,
    sem_as, sem_ar, sem_ps, sem_pr, sem_ss, sem_sr, sem_zs, sem_zr, sem_ys, sem_yr, sem_gs, sem_gr,
):
    nc = 2 * nz
    half_z = nz // 2
    me = lax.axis_index("ctx")
    y = lax.axis_index("head")
    x = lax.axis_index("dp")
    z = me // 2
    c = lax.rem(me, 2)
    sib = z * 2 + (1 - c)

    def at_z(off):
        return lax.rem(z + off + nz, nz)

    def rem_copy(src, dst, ssem, rsem, dev):
        return pltpu.make_async_remote_copy(
            src_ref=src, dst_ref=dst, send_sem=ssem, recv_sem=rsem, device_id=dev, device_id_type=MESH
        )

    ins = (x_in, kr_in, gain_in, pos_in, qn_in, ku_in, go_in, vu_in, qr_in)
    here = (x_ref, kr_ref, gain_ref, pos_ref, qn_ref, ku_ref, go_ref, vu_ref, qr_ref)
    loads = [pltpu.make_async_copy(a, b, sem_in.at[i]) for i, (a, b) in enumerate(zip(ins, here))]
    for load in loads[0:4]:
        load.start()

    barrier = pltpu.get_barrier_semaphore()
    for d in range(1, nc):
        pl.semaphore_signal(barrier, inc=1, device_id={"ctx": lax.rem(me + d, nc)}, device_id_type=MESH)
    for d in range(1, ny):
        pl.semaphore_signal(barrier, inc=1, device_id={"head": lax.rem(y + d, ny)}, device_id_type=MESH)
    for d in range(1, nx):
        pl.semaphore_signal(barrier, inc=1, device_id={"dp": lax.rem(x + d, nx)}, device_id_type=MESH)

    for load in loads[4:]:
        load.start()

    for load in loads[0:4]:
        load.wait()
    rows = x_ref[0].astype(F32)
    rms = jnp.sqrt(jnp.mean(rows * rows, axis=-1, keepdims=True) + 1e-06)
    keys[me, 0:128, :] = (rows / rms * gain_ref[...]).astype(BF16)
    ri = lax.broadcasted_iota(jnp.int32, (64, 128), 0)
    ci = lax.broadcasted_iota(jnp.int32, (64, 128), 1)
    rotary = kr_ref[0]
    none = jnp.zeros_like(rotary)
    packed = dot_t((ci == ri).astype(BF16), jnp.concatenate([rotary, none], axis=0)) + dot_t(
        (ci == ri + 64).astype(BF16), jnp.concatenate([none, rotary], axis=0)
    )
    packed = packed.astype(BF16)
    for g in range(4):
        keys[me, 128:144, 128 * g : 128 * g + 128] = packed[16 * g : 16 * g + 16]
    posbuf[me] = pos_ref[...]

    pl.semaphore_wait(barrier, (nc - 1) + (ny - 1) + (nx - 1))

    started = []

    def start(copy):
        copy.start()
        started.append(copy)

    offsets = [0] + [off for t in range(1, half_z) for off in (t, -t)] + [half_z]
    index_of = {off: i for i, off in enumerate(offsets)}
    far = [off for off in offsets if abs(off) > 1]

    def lanes(row):
        return pl.ds(pl.multiple_of(128 * lax.rem(row + ny, 4), 128), 128)

    def z_copy(off, owner):
        i = index_of[off]
        ref = keys.at[owner] if off not in far else keys.at[owner, :, lanes(y)]
        return rem_copy(ref, ref, sem_as.at[0, i], sem_ar.at[0, i], {"ctx": at_z(off) * 2 + c})

    def sib_block(off, core):
        i = index_of[off]
        ref = keys.at[at_z(off) * 2 + core]
        return rem_copy(ref, ref, sem_as.at[1, i], sem_ar.at[1, i], {"ctx": sib})

    def y_quarter(off, way, row):
        i = index_of[off]
        step = (1, -1, 2 - 4 * c)[way]
        ref = keys.at[at_z(off) * 2 + c, :, lanes(row)]
        return rem_copy(
            ref, ref, sem_as.at[2 + way, i], sem_ar.at[2 + way, i], {"head": lax.rem(y + step + ny, ny)}
        )

    def take_far(off):
        z_copy(-off if off != half_z else off, at_z(off) * 2 + c).wait_recv()
        for way in range(3):
            start(y_quarter(off, way, y))

    def take_rest(off):
        if off in far:
            for way in range(3):
                y_quarter(off, way, y - (1, -1, 2)[way]).wait_recv()
        else:
            z_copy(-off if off != half_z else off, at_z(off) * 2 + c).wait_recv()
        start(sib_block(off, c))

    def pos_copy(d, slot):
        return rem_copy(
            posbuf.at[slot], posbuf.at[slot], sem_ps.at[d], sem_pr.at[d], {"ctx": lax.rem(me + d, nc)}
        )

    for off in far:
        start(z_copy(off, me))
    start(sib_block(0, c))
    for d in range(1, nc):
        start(pos_copy(d, me))
    for off in offsets[1:3]:
        start(z_copy(off, me))

    fi = lax.broadcasted_iota(jnp.int32, (128, 128), 0)
    fj = lax.broadcasted_iota(jnp.int32, (128, 128), 1)
    for load in loads[4:]:
        load.wait()
    for h in range(8):
        part = dot(qn_ref[0, :, 128 * h : 128 * h + 128], ku_ref[h]).astype(BF16)
        qlat[0, 64 * h : 64 * h + 64, :] = part[0:64]
        qlat[1, 64 * h : 64 * h + 64, :] = part[64:128]
        part = dot(go_ref[0, :, 128 * h : 128 * h + 128], vu_ref[h]).astype(BF16)
        olat[0, 64 * h : 64 * h + 64, :] = part[0:64]
        olat[1, 64 * h : 64 * h + 64, :] = part[64:128]
        pair = qr_ref[0, :, 128 * (h // 2) : 128 * (h // 2) + 128]
        e = 64 * (h % 2)
        left = dot(pair, ((fi == fj + e) & (fj < 64)).astype(BF16)).astype(BF16)
        right = dot(pair[64:128], ((fi + 64 - e == fj) & (fj >= 64)).astype(BF16)).astype(BF16)
        qrp[0, 64 * h : 64 * h + 64, :] = left[0:64]
        qrp[1, 64 * h : 64 * h + 64, :] = left[64:128]
        qrp[2, 64 * h : 64 * h + 64, :] = right
    diff[...] = lax.rem(lax.broadcasted_iota(jnp.int32, (64, 512), 1), 64) - lax.broadcasted_iota(
        jnp.int32, (64, 512), 0
    )

    scale = float(128 + 64) ** (-0.5)
    to_log2 = scale * math.log2(math.e)

    groups = [[0]] + [[t, -t] for t in range(1, half_z)] + [[half_z]]
    first = []
    count = 0
    for g in groups:
        first.append(count)
        count += 2 * len(g)

    def blocks_of(g):
        return [at_z(off) * 2 + cc for off in g for cc in range(2)]

    def cat(parts):
        return parts[0] if len(parts) == 1 else jnp.concatenate(parts, axis=0)

    def rope_rows(b):
        return [keys[b, 128:144, 128 * g : 128 * g + 128] for g in range(4)]

    m_up = jnp.full((1, 512), -jnp.inf, F32)
    m_lo = m_up
    l_up = jnp.zeros((1, 512), F32)
    l_lo, d_up, d_lo = l_up, l_up, l_up
    tops = {}
    order = [0, 2, 1, 3, 4] if half_z == 4 else list(range(half_z + 1))
    for t in order:
        g = groups[t]
        if t == 0:
            for off in far[0:2]:
                take_far(off)
            pos_copy(jnp.where(c == 1, 1, nc - 1), sib).wait_recv()
        else:
            if t == order[1]:
                for off in far[2:]:
                    take_far(off)
                for d in range(2, nc - 1):
                    pos_copy(d, lax.rem(me - d + nc, nc)).wait_recv()
                d = jnp.where(c == 1, nc - 1, 1)
                pos_copy(d, lax.rem(me - d + nc, nc)).wait_recv()
            ahead = {1: [1, 3], 3: [4], 4: []} if half_z == 4 else {}
            for other in ahead.get(t, [t]):
                for off in groups[other]:
                    take_rest(off)
        for off in g:
            sib_block(off, 1 - c).wait_recv()

        blocks = blocks_of(g)
        n = 64 * len(blocks)
        span = pl.ds(64 * first[t], n)
        low = cat([keys[b, 0:64, :] for b in blocks])
        high = cat([keys[b, 64:128, :] for b in blocks])
        rope = cat([r for b in blocks for r in rope_rows(b)])
        wbuf[0, span, :] = (dot_t(low, qlat[1]) + dot_t(rope, qrp[1])) * to_log2
        dbuf[0, span, :] = dot_t(low, olat[1])
        s_high = (dot_t(high, qlat[1]) + dot_t(rope, qrp[2])) * to_log2
        dbuf[1, span, :] = dot_t(high, olat[1])
        s_low = (dot_t(low, qlat[0]) + dot_t(rope, qrp[0])) * to_log2
        dbuf[2, span, :] = dot_t(low, olat[0])
        for i, b in enumerate(blocks):
            sub = pl.ds(64 * (first[t] + i), 64)
            late = posbuf[b, 0:1, 64:65] - pos_ref[0:1, 64:65]
            early = posbuf[b, 0:1, 0:1] - pos_ref[0:1, 0:1]
            wbuf[1, sub, :] = jnp.where(diff[...] >= late, s_high[64 * i : 64 * i + 64], -jnp.inf)
            wbuf[2, sub, :] = jnp.where(diff[...] >= early, s_low[64 * i : 64 * i + 64], -jnp.inf)
        new_up = jnp.maximum(
            m_up,
            jnp.maximum(
                jnp.max(wbuf[0, span, :], axis=0, keepdims=True), jnp.max(wbuf[1, span, :], axis=0, keepdims=True)
            ),
        )
        new_lo = jnp.maximum(m_lo, jnp.max(wbuf[2, span, :], axis=0, keepdims=True))
        a_up = jnp.exp2(m_up - new_up)
        a_lo = jnp.exp2(m_lo - new_lo)
        m_up, m_lo = new_up, new_lo
        l_up, d_up, l_lo, d_lo = l_up * a_up, d_up * a_up, l_lo * a_lo, d_lo * a_lo
        tops[t] = (m_up, m_lo)
        for kind in range(3):
            top = m_lo if kind == 2 else m_up
            w = jnp.exp2(wbuf[kind, span, :] - top)
            wbuf[kind, span, :] = w
            l_add = jnp.sum(w, axis=0, keepdims=True)
            d_add = jnp.sum(w * dbuf[kind, span, :], axis=0, keepdims=True)
            if kind == 2:
                l_lo, d_lo = l_lo + l_add, d_lo + d_add
            else:
                l_up, d_up = l_up + l_add, d_up + d_add

    inv_up, inv_lo = 1.0 / l_up, 1.0 / l_lo
    delta_up, delta_lo = d_up * inv_up, d_lo * inv_lo

    def sib_copy(index):
        return rem_copy(
            psib.at[index], rsib.at[index], sem_ss.at[index], sem_sr.at[index], {"ctx": sib}
        )

    relayed = half_z == 4
    stops = {3: 1, -3: -1, 4: 2 - 4 * c} if relayed else {}

    def z_part(i):
        off = offsets[i]
        return rem_copy(
            zout.at[i], zin.at[i], sem_zs.at[0, i], sem_zr.at[0, i], {"ctx": at_z(stops.get(off, off)) * 2 + c}
        )

    def relay():
        for off in (3, -3, 4):
            z_part(index_of[off]).wait_recv()
        for off, source, core in ((2, 3, 0), (-2, -3, 1)):
            i = index_of[off]
            total = pown[i, 0:160].astype(F32) + rsib[i, 0:160].astype(F32) + zin[index_of[source]].astype(F32)
            zout[i] = (total + jnp.where(c == core, zin[index_of[4]].astype(F32), 0.0)).astype(BF16)
            start(z_part(i))

    cuts = [[t] for t in range(half_z, -1, -1)]

    def y_part(k, d):
        begin = index_of[groups[cuts[k][0]][0]]
        size = sum(len(groups[t]) for t in cuts[k])
        peer = lax.rem(y + d, ny)
        stop = lax.rem(y + {3: 1, 5: 7, 4: 2 + 4 * c}.get(d, d), ny) if y_relayed(k) else peer
        return rem_copy(
            yout.at[peer, pl.ds(begin, size)], yin.at[d - 1, pl.ds(begin, size)],
            sem_ys.at[k, d], sem_yr.at[k, d], {"head": stop},
        )

    def y_relayed(k):
        return ny == 8 and cuts[k][0] > 1

    def y_relay(k):
        begin = index_of[groups[cuts[k][0]][0]]
        span = pl.ds(begin, sum(len(groups[t]) for t in cuts[k]))
        for d in (3, 5, 4):
            y_part(k, d).wait_recv()
        for d, source, core in ((2, 3, 0), (6, 5, 1)):
            peer = lax.rem(y + d, ny)
            total = yout[peer, span].astype(F32) + yin[source - 1, span].astype(F32)
            yout[peer, span] = (total + jnp.where(c == core, yin[3, span].astype(F32), 0.0)).astype(BF16)
            start(y_part(k, d))

    def send_on(t):
        for off in groups[t]:
            i = index_of[off]
            sib_copy(i).wait_recv()
            total = (pown[i].astype(F32) + rsib[i].astype(F32)).astype(BF16)
            if not relayed or abs(off) != 2:
                zout[i] = total[0:160]
                if off != 0:
                    start(z_part(i))
            for k in range(ny):
                yout[k, i] = total[160 + 16 * k : 176 + 16 * k]
        for k, cut in enumerate(cuts):
            if cut[0] == t:
                for d in range(1, ny):
                    if not (y_relayed(k) and d in (2, 6)):
                        start(y_part(k, d))

    gain_acc = jnp.zeros((1, 512), F32)
    for t in reversed(range(len(groups))):
        g = groups[t]
        blocks = blocks_of(g)
        n = 64 * len(blocks)
        span = pl.ds(64 * first[t], n)
        c_up = jnp.exp2(tops[t][0] - m_up) * inv_up
        c_lo = jnp.exp2(tops[t][1] - m_lo) * inv_lo
        probs = []
        dscores = []
        for kind in range(3):
            factor, delta = (c_lo, delta_lo) if kind == 2 else (c_up, delta_up)
            p = wbuf[kind, span, :] * factor
            probs.append(p.astype(BF16))
            dscores.append((p * (dbuf[kind, span, :] - delta) * scale).astype(BF16))
        lat_low = (
            dot(probs[0], olat[1]) + dot(dscores[0], qlat[1]) + dot(probs[2], olat[0]) + dot(dscores[2], qlat[0])
        )
        lat_high = dot(probs[1], olat[1]) + dot(dscores[1], qlat[1])
        rope = dot(dscores[0], qrp[1]) + dot(dscores[1], qrp[2]) + dot(dscores[2], qrp[0])
        low = cat([keys[b, 0:64, :] for b in blocks])
        high = cat([keys[b, 64:128, :] for b in blocks])
        gain_acc = gain_acc + jnp.sum(
            lat_low * low.astype(F32) + lat_high * high.astype(F32), axis=0, keepdims=True
        )
        lat_low = lat_low.astype(BF16)
        lat_high = lat_high.astype(BF16)
        rope = rope.astype(BF16)
        for i, b in enumerate(blocks):
            index = index_of[g[i // 2]]

            def put(buf):
                buf[index, 0:64, :] = lat_low[64 * i : 64 * i + 64, 0:256]
                buf[index, 64:128, :] = lat_high[64 * i : 64 * i + 64, 0:256]
                for k in range(4):
                    buf[index, 128 + 16 * (k // 2) : 144 + 16 * (k // 2), 128 * (k % 2) : 128 * (k % 2) + 128] = rope[
                        64 * i + 16 * k : 64 * i + 16 * k + 16
                    ]
                buf[index, 160:224, :] = lat_low[64 * i : 64 * i + 64, 256:512]
                buf[index, 224:288, :] = lat_high[64 * i : 64 * i + 64, 256:512]

            @pl.when(c == i % 2)
            def _():
                put(pown)

            @pl.when(c != i % 2)
            def _():
                put(psib)

        for off in g:
            start(sib_copy(index_of[off]))
        if t < half_z:
            send_on(t + 1)

    gsend[0] = gain_acc

    def gain_copy(stage, d, slot):
        buf, base, axis, pos, size = (
            (gx, 0, "dp", x, nx), (gy, nx - 1, "head", y, ny), (gc, nx + ny - 2, "ctx", me, nc)
        )[stage]
        return rem_copy(
            gsend.at[stage], buf.at[slot], sem_gs.at[base + d - 1], sem_gr.at[base + d - 1],
            {axis: lax.rem(pos + d, size)},
        )

    def gain_send(stage):
        buf, pos, size = ((gx, x, nx), (gy, y, ny), (gc, me, nc))[stage]
        buf[pos] = gsend[stage]
        for d in range(1, size):
            start(gain_copy(stage, d, pos))

    def gain_sum(stage):
        buf, pos, size = ((gx, x, nx), (gy, y, ny), (gc, me, nc))[stage]
        for d in range(1, size):
            gain_copy(stage, d, lax.rem(pos - d + size, size)).wait_recv()
        return jnp.sum(buf[...], axis=0)

    gain_send(0)
    send_on(0)
    if y_relayed(0):
        y_relay(0)
    gsend[1] = gain_sum(0)
    gain_send(1)
    if relayed:
        relay()
    for k in range(1, len(cuts)):
        if y_relayed(k):
            y_relay(k)
    gsend[2] = gain_sum(1)
    gain_send(2)

    total = zout[0].astype(F32)
    for i in range(1, nz):
        if offsets[i] not in stops:
            z_part(i).wait_recv()
            total = total + zin[i].astype(F32)
    total = total.astype(BF16)
    for k in range(ny):
        q = k % 4
        yout2[k, :, 0:256] = total[16 * k : 16 * k + 16]
        yout2[k, :, 256:384] = total[128 + 16 * (q // 2) : 144 + 16 * (q // 2), 128 * (q % 2) : 128 * (q % 2) + 128]

    def y_last(d):
        peer = lax.rem(y + d, ny)
        return rem_copy(yout2.at[peer], yin2.at[d], sem_ys.at[half_z + 1, d], sem_yr.at[half_z + 1, d], {"head": peer})

    for d in range(1, ny):
        start(y_last(d))

    def z_last(i):
        return rem_copy(
            zout2.at[i], zin2.at[i], sem_zs.at[1, i], sem_zr.at[1, i], {"ctx": at_z(offsets[i]) * 2 + c}
        )

    for k, cut in enumerate(cuts):
        begin = index_of[groups[cut[0]][0]]
        span = pl.ds(begin, sum(len(groups[t]) for t in cut))
        right = yout[y, span].astype(F32)
        for d in range(1, ny):
            if not (y_relayed(k) and d in (3, 4, 5)):
                y_part(k, d).wait_recv()
                right = right + yin[d - 1, span].astype(F32)
        zout2[span] = right.astype(BF16)
    for i in range(1, nz):
        start(z_last(i))

    left = yout2[y].astype(F32)
    for d in range(1, ny):
        y_last(d).wait_recv()
        left = left + yin2[d].astype(F32)
    right = zout2[0].astype(F32)
    for i in range(1, nz):
        z_last(i).wait_recv()
        right = right + zin2[i].astype(F32)

    cot = jnp.concatenate([left[:, 0:256], right], axis=1)
    own = x_ref[0, pl.ds(pl.multiple_of(16 * y, 16), 16), :].astype(F32)
    own_rms = jnp.sqrt(jnp.mean(own * own, axis=-1, keepdims=True) + 1e-06)
    xhat = own / own_rms
    scaled = gain_ref[...] * cot
    raw_ref[0] = (scaled - xhat * jnp.mean(scaled * xhat, axis=-1, keepdims=True)) / own_rms
    both = left[:, 256:384]
    rope_ref[0] = jnp.where(y >= ny // 2, pltpu.roll(both, 64, 1), both)[:, 0:64]

    gout_ref[...] = gain_sum(2) / gain_ref[...] * (1.0 / math.sqrt(total_rows))
    for copy in started:
        copy.wait_send()


def hand_over(raw_in, rope_in, gain_in, raw_out, rope_out, gain_out):
    raw_out[...] = raw_in[...]
    rope_out[...] = rope_in[...]
    gain_out[...] = gain_in[...]


def solution(mesh):
    nc, ny, nx = mesh.shape["ctx"], mesh.shape["head"], mesh.shape["dp"]
    nz = nc // 2
    half_z = nz // 2

    def per_device(pos, unnormed, gain, kr, qn, qr, ku, vu, go):
        dma = pltpu.SemaphoreType.DMA
        out = pl.pallas_call(
            functools.partial(kernel, nz, ny, nx, nc * 128 * nx),
            out_shape=(
                jax.ShapeDtypeStruct((1, 16, 512), F32),
                jax.ShapeDtypeStruct((1, 16, 64), F32),
                jax.ShapeDtypeStruct((1, 512), F32),
            ),
            in_specs=[pl.BlockSpec(memory_space=pltpu.HBM)] * 9,
            out_specs=[pl.BlockSpec(memory_space=pltpu.VMEM)] * 3,
            scratch_shapes=[
                pltpu.VMEM((1, 128), jnp.int32),
                pltpu.VMEM((1, 128, 512), BF16),
                pltpu.VMEM((1, 512), F32),
                pltpu.VMEM((1, 64, 128), BF16),
                pltpu.VMEM((1, 128, 1024), BF16),
                pltpu.VMEM((1, 128, 512), BF16),
                pltpu.VMEM((8, 128, 512), BF16),
                pltpu.VMEM((8, 128, 512), BF16),
                pltpu.VMEM((1, 128, 1024), BF16),
                dma((9,)),
                pltpu.VMEM((nc, 144, 512), BF16),
                pltpu.VMEM((nc, 1, 128), jnp.int32),
                pltpu.VMEM((2, 512, 512), BF16),
                pltpu.VMEM((2, 512, 512), BF16),
                pltpu.VMEM((3, 512, 128), BF16),
                pltpu.VMEM((3, 64 * nc, 512), F32),
                pltpu.VMEM((3, 64 * nc, 512), F32),
                pltpu.VMEM((64, 512), jnp.int32),
                pltpu.VMEM((nz, 288, 256), BF16),
                pltpu.VMEM((nz, 288, 256), BF16),
                pltpu.VMEM((nz, 288, 256), BF16),
                pltpu.VMEM((nz, 160, 256), BF16),
                pltpu.VMEM((nz, 160, 256), BF16),
                pltpu.VMEM((ny, nz, 16, 256), BF16),
                pltpu.VMEM((ny, nz, 16, 256), BF16),
                pltpu.VMEM((ny, 16, 384), BF16),
                pltpu.VMEM((ny, 16, 384), BF16),
                pltpu.VMEM((nz, 16, 256), BF16),
                pltpu.VMEM((nz, 16, 256), BF16),
                pltpu.VMEM((3, 1, 512), F32),
                pltpu.VMEM((nx, 1, 512), F32),
                pltpu.VMEM((ny, 1, 512), F32),
                pltpu.VMEM((nc, 1, 512), F32),
                dma((5, nz)),
                dma((5, nz)),
                dma((nc,)),
                dma((nc,)),
                dma((nz,)),
                dma((nz,)),
                dma((2, nz)),
                dma((2, nz)),
                dma((half_z + 2, ny)),
                dma((half_z + 2, ny)),
                dma((nx + ny + nc,)),
                dma((nx + ny + nc,)),
            ],
            compiler_params=pltpu.CompilerParams(
                collective_id=0, has_side_effects=True, vmem_limit_bytes=60 * 1024 * 1024
            ),
        )(pos, unnormed, gain.reshape(1, 512), jnp.swapaxes(kr, 1, 2), qn, qr, ku, vu, go)
        out = pl.pallas_call(
            hand_over,
            out_shape=tuple(jax.ShapeDtypeStruct(o.shape, F32) for o in out),
            in_specs=[pl.BlockSpec(memory_space=pltpu.VMEM)] * 3,
            out_specs=[pl.BlockSpec(memory_space=pltpu.VMEM)] * 3,
        )(*out)
        return out[0], out[1], out[2].reshape(512)

    in_specs = (
        P("dp", "ctx"),
        P("dp", "ctx", None),
        P(),
        P("dp", "ctx", None),
        P("dp", "ctx", "head"),
        P("dp", "ctx", "head"),
        P("head", None, None),
        P("head", None, None),
        P("dp", "ctx", "head"),
    )
    out_specs = (P("dp", ("ctx", "head"), None), P("dp", ("ctx", "head"), None), P())
    return jax.shard_map(
        per_device, mesh=mesh, in_specs=in_specs, out_specs=out_specs, check_vma=False
    )
```

```python
import functools
import math

import jax
import jax.numpy as jnp
from jax import lax
from jax.experimental import pallas as pl
from jax.experimental.pallas import tpu as pltpu
from jax.sharding import PartitionSpec as P

BF16 = jnp.bfloat16
F32 = jnp.float32
MESH = pl.DeviceIdType.MESH


def dot(a, b):
    return jnp.dot(a, b, preferred_element_type=F32)


def dot_t(a, b):
    return lax.dot_general(a, b, (((1,), (1,)), ((), ())), preferred_element_type=F32)


def kernel(
    nz, ny, nx, total_rows,
    pos_in, x_in, gain_in, kr_in, qn_in, qr_in, ku_in, vu_in, go_in,
    raw_ref, rope_ref, gout_ref,
    pos_ref, x_ref, gain_ref, kr_ref, qn_ref, qr_ref, ku_ref, vu_ref, go_ref, sem_in,
    keys, posbuf, qlat, olat, qrp, wbuf, dbuf, diff,
    pown, psib, rsib, zout, zin, yout, yin, yout2, yin2, zout2, zin2, gsend, gx, gy, gc,
    sem_as, sem_ar, sem_ps, sem_pr, sem_ss, sem_sr, sem_zs, sem_zr, sem_ys, sem_yr, sem_gs, sem_gr,
):
    nc = 2 * nz
    half_z = nz // 2
    me = lax.axis_index("ctx")
    y = lax.axis_index("head")
    x = lax.axis_index("dp")
    z = me // 2
    c = lax.rem(me, 2)
    sib = z * 2 + (1 - c)

    def at_z(off):
        return lax.rem(z + off + nz, nz)

    def rem_copy(src, dst, ssem, rsem, dev):
        return pltpu.make_async_remote_copy(
            src_ref=src, dst_ref=dst, send_sem=ssem, recv_sem=rsem, device_id=dev, device_id_type=MESH
        )

    ins = (x_in, kr_in, gain_in, pos_in, qn_in, ku_in, go_in, vu_in, qr_in)
    here = (x_ref, kr_ref, gain_ref, pos_ref, qn_ref, ku_ref, go_ref, vu_ref, qr_ref)
    loads = [pltpu.make_async_copy(a, b, sem_in.at[i]) for i, (a, b) in enumerate(zip(ins, here))]
    for load in loads[0:4]:
        load.start()

    barrier = pltpu.get_barrier_semaphore()
    for d in range(1, nc):
        pl.semaphore_signal(barrier, inc=1, device_id={"ctx": lax.rem(me + d, nc)}, device_id_type=MESH)
    for d in range(1, ny):
        pl.semaphore_signal(barrier, inc=1, device_id={"head": lax.rem(y + d, ny)}, device_id_type=MESH)
    for d in range(1, nx):
        pl.semaphore_signal(barrier, inc=1, device_id={"dp": lax.rem(x + d, nx)}, device_id_type=MESH)

    for load in loads[4:]:
        load.start()

    for load in loads[0:4]:
        load.wait()
    rows = x_ref[0].astype(F32)
    rms = jnp.sqrt(jnp.mean(rows * rows, axis=-1, keepdims=True) + 1e-06)
    keys[me, 0:128, :] = (rows / rms * gain_ref[...]).astype(BF16)
    ri = lax.broadcasted_iota(jnp.int32, (64, 128), 0)
    ci = lax.broadcasted_iota(jnp.int32, (64, 128), 1)
    rotary = kr_ref[0]
    none = jnp.zeros_like(rotary)
    packed = dot_t((ci == ri).astype(BF16), jnp.concatenate([rotary, none], axis=0)) + dot_t(
        (ci == ri + 64).astype(BF16), jnp.concatenate([none, rotary], axis=0)
    )
    packed = packed.astype(BF16)
    for g in range(4):
        keys[me, 128:144, 128 * g : 128 * g + 128] = packed[16 * g : 16 * g + 16]
    posbuf[me] = pos_ref[...]

    pl.semaphore_wait(barrier, (nc - 1) + (ny - 1) + (nx - 1))

    started = []

    def start(copy):
        copy.start()
        started.append(copy)

    offsets = [0] + [off for t in range(1, half_z) for off in (t, -t)] + [half_z]
    index_of = {off: i for i, off in enumerate(offsets)}
    far = [off for off in offsets if abs(off) > 1]

    def lanes(row):
        return pl.ds(pl.multiple_of(128 * lax.rem(row + ny, 4), 128), 128)

    def z_copy(off, owner):
        i = index_of[off]
        ref = keys.at[owner] if off not in far else keys.at[owner, :, lanes(y)]
        return rem_copy(ref, ref, sem_as.at[0, i], sem_ar.at[0, i], {"ctx": at_z(off) * 2 + c})

    def sib_block(off, core):
        i = index_of[off]
        ref = keys.at[at_z(off) * 2 + core]
        return rem_copy(ref, ref, sem_as.at[1, i], sem_ar.at[1, i], {"ctx": sib})

    def y_quarter(off, way, row):
        i = index_of[off]
        step = (1, -1, 2 - 4 * c)[way]
        ref = keys.at[at_z(off) * 2 + c, :, lanes(row)]
        return rem_copy(
            ref, ref, sem_as.at[2 + way, i], sem_ar.at[2 + way, i], {"head": lax.rem(y + step + ny, ny)}
        )

    def take_far(off):
        z_copy(-off if off != half_z else off, at_z(off) * 2 + c).wait_recv()
        for way in range(3):
            start(y_quarter(off, way, y))

    def take_rest(off):
        if off in far:
            for way in range(3):
                y_quarter(off, way, y - (1, -1, 2)[way]).wait_recv()
        else:
            z_copy(-off if off != half_z else off, at_z(off) * 2 + c).wait_recv()
        start(sib_block(off, c))

    def pos_copy(d, slot):
        return rem_copy(
            posbuf.at[slot], posbuf.at[slot], sem_ps.at[d], sem_pr.at[d], {"ctx": lax.rem(me + d, nc)}
        )

    for off in far:
        start(z_copy(off, me))
    start(sib_block(0, c))
    for d in range(1, nc):
        start(pos_copy(d, me))
    for off in offsets[1:3]:
        start(z_copy(off, me))

    fi = lax.broadcasted_iota(jnp.int32, (128, 128), 0)
    fj = lax.broadcasted_iota(jnp.int32, (128, 128), 1)
    for load in loads[4:]:
        load.wait()
    for h in range(8):
        part = dot(qn_ref[0, :, 128 * h : 128 * h + 128], ku_ref[h]).astype(BF16)
        qlat[0, 64 * h : 64 * h + 64, :] = part[0:64]
        qlat[1, 64 * h : 64 * h + 64, :] = part[64:128]
        part = dot(go_ref[0, :, 128 * h : 128 * h + 128], vu_ref[h]).astype(BF16)
        olat[0, 64 * h : 64 * h + 64, :] = part[0:64]
        olat[1, 64 * h : 64 * h + 64, :] = part[64:128]
        pair = qr_ref[0, :, 128 * (h // 2) : 128 * (h // 2) + 128]
        e = 64 * (h % 2)
        left = dot(pair, ((fi == fj + e) & (fj < 64)).astype(BF16)).astype(BF16)
        right = dot(pair[64:128], ((fi + 64 - e == fj) & (fj >= 64)).astype(BF16)).astype(BF16)
        qrp[0, 64 * h : 64 * h + 64, :] = left[0:64]
        qrp[1, 64 * h : 64 * h + 64, :] = left[64:128]
        qrp[2, 64 * h : 64 * h + 64, :] = right
    diff[...] = lax.rem(lax.broadcasted_iota(jnp.int32, (64, 512), 1), 64) - lax.broadcasted_iota(
        jnp.int32, (64, 512), 0
    )

    scale = float(128 + 64) ** (-0.5)
    to_log2 = scale * math.log2(math.e)

    groups = [[0]] + [[t, -t] for t in range(1, half_z)] + [[half_z]]
    first = []
    count = 0
    for g in groups:
        first.append(count)
        count += 2 * len(g)

    def blocks_of(g):
        return [at_z(off) * 2 + cc for off in g for cc in range(2)]

    def cat(parts):
        return parts[0] if len(parts) == 1 else jnp.concatenate(parts, axis=0)

    def rope_rows(b):
        return [keys[b, 128:144, 128 * g : 128 * g + 128] for g in range(4)]

    m_up = jnp.full((1, 512), -jnp.inf, F32)
    m_lo = m_up
    l_up = jnp.zeros((1, 512), F32)
    l_lo, d_up, d_lo = l_up, l_up, l_up
    tops = {}
    order = [0, 2, 1, 3, 4] if half_z == 4 else list(range(half_z + 1))
    for t in order:
        g = groups[t]
        if t == 0:
            for off in far[0:2]:
                take_far(off)
            pos_copy(jnp.where(c == 1, 1, nc - 1), sib).wait_recv()
        else:
            if t == order[1]:
                for off in far[2:]:
                    take_far(off)
                for d in range(2, nc - 1):
                    pos_copy(d, lax.rem(me - d + nc, nc)).wait_recv()
                d = jnp.where(c == 1, nc - 1, 1)
                pos_copy(d, lax.rem(me - d + nc, nc)).wait_recv()
            ahead = {1: [1, 3], 3: [4], 4: []} if half_z == 4 else {}
            for other in ahead.get(t, [t]):
                for off in groups[other]:
                    take_rest(off)
        for off in g:
            sib_block(off, 1 - c).wait_recv()

        blocks = blocks_of(g)
        n = 64 * len(blocks)
        span = pl.ds(64 * first[t], n)
        low = cat([keys[b, 0:64, :] for b in blocks])
        high = cat([keys[b, 64:128, :] for b in blocks])
        rope = cat([r for b in blocks for r in rope_rows(b)])
        wbuf[0, span, :] = (dot_t(low, qlat[1]) + dot_t(rope, qrp[1])) * to_log2
        dbuf[0, span, :] = dot_t(low, olat[1])
        s_high = (dot_t(high, qlat[1]) + dot_t(rope, qrp[2])) * to_log2
        dbuf[1, span, :] = dot_t(high, olat[1])
        s_low = (dot_t(low, qlat[0]) + dot_t(rope, qrp[0])) * to_log2
        dbuf[2, span, :] = dot_t(low, olat[0])
        for i, b in enumerate(blocks):
            sub = pl.ds(64 * (first[t] + i), 64)
            late = posbuf[b, 0:1, 64:65] - pos_ref[0:1, 64:65]
            early = posbuf[b, 0:1, 0:1] - pos_ref[0:1, 0:1]
            wbuf[1, sub, :] = jnp.where(diff[...] >= late, s_high[64 * i : 64 * i + 64], -jnp.inf)
            wbuf[2, sub, :] = jnp.where(diff[...] >= early, s_low[64 * i : 64 * i + 64], -jnp.inf)
        new_up = jnp.maximum(
            m_up,
            jnp.maximum(
                jnp.max(wbuf[0, span, :], axis=0, keepdims=True), jnp.max(wbuf[1, span, :], axis=0, keepdims=True)
            ),
        )
        new_lo = jnp.maximum(m_lo, jnp.max(wbuf[2, span, :], axis=0, keepdims=True))
        a_up = jnp.exp2(m_up - new_up)
        a_lo = jnp.exp2(m_lo - new_lo)
        m_up, m_lo = new_up, new_lo
        l_up, d_up, l_lo, d_lo = l_up * a_up, d_up * a_up, l_lo * a_lo, d_lo * a_lo
        tops[t] = (m_up, m_lo)
        for kind in range(3):
            top = m_lo if kind == 2 else m_up
            w = jnp.exp2(wbuf[kind, span, :] - top)
            wbuf[kind, span, :] = w
            l_add = jnp.sum(w, axis=0, keepdims=True)
            d_add = jnp.sum(w * dbuf[kind, span, :], axis=0, keepdims=True)
            if kind == 2:
                l_lo, d_lo = l_lo + l_add, d_lo + d_add
            else:
                l_up, d_up = l_up + l_add, d_up + d_add

    inv_up, inv_lo = 1.0 / l_up, 1.0 / l_lo
    delta_up, delta_lo = d_up * inv_up, d_lo * inv_lo

    def sib_copy(index):
        return rem_copy(
            psib.at[index], rsib.at[index], sem_ss.at[index], sem_sr.at[index], {"ctx": sib}
        )

    relayed = half_z == 4
    stops = {3: 1, -3: -1, 4: 2 - 4 * c} if relayed else {}

    def z_part(i):
        off = offsets[i]
        return rem_copy(
            zout.at[i], zin.at[i], sem_zs.at[0, i], sem_zr.at[0, i], {"ctx": at_z(stops.get(off, off)) * 2 + c}
        )

    def relay():
        for off in (3, -3, 4):
            z_part(index_of[off]).wait_recv()
        for off, source, core in ((2, 3, 0), (-2, -3, 1)):
            i = index_of[off]
            total = pown[i, 0:160].astype(F32) + rsib[i, 0:160].astype(F32) + zin[index_of[source]].astype(F32)
            zout[i] = (total + jnp.where(c == core, zin[index_of[4]].astype(F32), 0.0)).astype(BF16)
            start(z_part(i))

    cuts = [[t] for t in range(half_z, -1, -1)]

    def y_part(k, d):
        begin = index_of[groups[cuts[k][0]][0]]
        size = sum(len(groups[t]) for t in cuts[k])
        peer = lax.rem(y + d, ny)
        stop = lax.rem(y + {3: 1, 5: 7, 4: 2 + 4 * c}.get(d, d), ny) if y_relayed(k) else peer
        return rem_copy(
            yout.at[peer, pl.ds(begin, size)], yin.at[d - 1, pl.ds(begin, size)],
            sem_ys.at[k, d], sem_yr.at[k, d], {"head": stop},
        )

    def y_relayed(k):
        return ny == 8 and cuts[k][0] > 1

    def y_relay(k):
        begin = index_of[groups[cuts[k][0]][0]]
        span = pl.ds(begin, sum(len(groups[t]) for t in cuts[k]))
        for d in (3, 5, 4):
            y_part(k, d).wait_recv()
        for d, source, core in ((2, 3, 0), (6, 5, 1)):
            peer = lax.rem(y + d, ny)
            total = yout[peer, span].astype(F32) + yin[source - 1, span].astype(F32)
            yout[peer, span] = (total + jnp.where(c == core, yin[3, span].astype(F32), 0.0)).astype(BF16)
            start(y_part(k, d))

    def send_on(t):
        for off in groups[t]:
            i = index_of[off]
            sib_copy(i).wait_recv()
            total = (pown[i].astype(F32) + rsib[i].astype(F32)).astype(BF16)
            if not relayed or abs(off) != 2:
                zout[i] = total[0:160]
                if off != 0:
                    start(z_part(i))
            for k in range(ny):
                yout[k, i] = total[160 + 16 * k : 176 + 16 * k]
        for k, cut in enumerate(cuts):
            if cut[0] == t:
                for d in range(1, ny):
                    if not (y_relayed(k) and d in (2, 6)):
                        start(y_part(k, d))

    gain_acc = jnp.zeros((1, 512), F32)
    for t in reversed(range(len(groups))):
        g = groups[t]
        blocks = blocks_of(g)
        n = 64 * len(blocks)
        span = pl.ds(64 * first[t], n)
        c_up = jnp.exp2(tops[t][0] - m_up) * inv_up
        c_lo = jnp.exp2(tops[t][1] - m_lo) * inv_lo
        probs = []
        dscores = []
        for kind in range(3):
            factor, delta = (c_lo, delta_lo) if kind == 2 else (c_up, delta_up)
            p = wbuf[kind, span, :] * factor
            probs.append(p.astype(BF16))
            dscores.append((p * (dbuf[kind, span, :] - delta) * scale).astype(BF16))
        lat_low = (
            dot(probs[0], olat[1]) + dot(dscores[0], qlat[1]) + dot(probs[2], olat[0]) + dot(dscores[2], qlat[0])
        )
        lat_high = dot(probs[1], olat[1]) + dot(dscores[1], qlat[1])
        rope = dot(dscores[0], qrp[1]) + dot(dscores[1], qrp[2]) + dot(dscores[2], qrp[0])
        low = cat([keys[b, 0:64, :] for b in blocks])
        high = cat([keys[b, 64:128, :] for b in blocks])
        gain_acc = gain_acc + jnp.sum(
            lat_low * low.astype(F32) + lat_high * high.astype(F32), axis=0, keepdims=True
        )
        lat_low = lat_low.astype(BF16)
        lat_high = lat_high.astype(BF16)
        rope = rope.astype(BF16)
        for i, b in enumerate(blocks):
            index = index_of[g[i // 2]]

            def put(buf):
                buf[index, 0:64, :] = lat_low[64 * i : 64 * i + 64, 0:256]
                buf[index, 64:128, :] = lat_high[64 * i : 64 * i + 64, 0:256]
                for k in range(4):
                    buf[index, 128 + 16 * (k // 2) : 144 + 16 * (k // 2), 128 * (k % 2) : 128 * (k % 2) + 128] = rope[
                        64 * i + 16 * k : 64 * i + 16 * k + 16
                    ]
                buf[index, 160:224, :] = lat_low[64 * i : 64 * i + 64, 256:512]
                buf[index, 224:288, :] = lat_high[64 * i : 64 * i + 64, 256:512]

            @pl.when(c == i % 2)
            def _():
                put(pown)

            @pl.when(c != i % 2)
            def _():
                put(psib)

        for off in g:
            start(sib_copy(index_of[off]))
        if t < half_z:
            send_on(t + 1)

    gsend[0] = gain_acc

    def gain_copy(stage, d, slot):
        buf, base, axis, pos, size = (
            (gx, 0, "dp", x, nx), (gy, nx - 1, "head", y, ny), (gc, nx + ny - 2, "ctx", me, nc)
        )[stage]
        return rem_copy(
            gsend.at[stage], buf.at[slot], sem_gs.at[base + d - 1], sem_gr.at[base + d - 1],
            {axis: lax.rem(pos + d, size)},
        )

    def gain_send(stage):
        buf, pos, size = ((gx, x, nx), (gy, y, ny), (gc, me, nc))[stage]
        buf[pos] = gsend[stage]
        for d in range(1, size):
            start(gain_copy(stage, d, pos))

    def gain_sum(stage):
        buf, pos, size = ((gx, x, nx), (gy, y, ny), (gc, me, nc))[stage]
        for d in range(1, size):
            gain_copy(stage, d, lax.rem(pos - d + size, size)).wait_recv()
        return jnp.sum(buf[...], axis=0)

    gain_send(0)
    send_on(0)
    if y_relayed(0):
        y_relay(0)
    if relayed:
        relay()
    for k in range(1, len(cuts)):
        if y_relayed(k):
            y_relay(k)
        if k == 1:
            gsend[1] = gain_sum(0)
            gain_send(1)
    gsend[2] = gain_sum(1)
    gain_send(2)

    total = zout[0].astype(F32)
    for i in range(1, nz):
        if offsets[i] not in stops:
            z_part(i).wait_recv()
            total = total + zin[i].astype(F32)
    total = total.astype(BF16)
    for k in range(ny):
        q = k % 4
        yout2[k, :, 0:256] = total[16 * k : 16 * k + 16]
        yout2[k, :, 256:384] = total[128 + 16 * (q // 2) : 144 + 16 * (q // 2), 128 * (q % 2) : 128 * (q % 2) + 128]

    def y_last(d):
        peer = lax.rem(y + d, ny)
        return rem_copy(yout2.at[peer], yin2.at[d], sem_ys.at[half_z + 1, d], sem_yr.at[half_z + 1, d], {"head": peer})

    for d in range(1, ny):
        start(y_last(d))

    def z_last(i):
        return rem_copy(
            zout2.at[i], zin2.at[i], sem_zs.at[1, i], sem_zr.at[1, i], {"ctx": at_z(offsets[i]) * 2 + c}
        )

    for k, cut in enumerate(cuts):
        begin = index_of[groups[cut[0]][0]]
        span = pl.ds(begin, sum(len(groups[t]) for t in cut))
        right = yout[y, span].astype(F32)
        for d in range(1, ny):
            if not (y_relayed(k) and d in (3, 4, 5)):
                y_part(k, d).wait_recv()
                right = right + yin[d - 1, span].astype(F32)
        zout2[span] = right.astype(BF16)
    for i in range(1, nz):
        start(z_last(i))

    left = yout2[y].astype(F32)
    for d in range(1, ny):
        y_last(d).wait_recv()
        left = left + yin2[d].astype(F32)
    right = zout2[0].astype(F32)
    for i in range(1, nz):
        z_last(i).wait_recv()
        right = right + zin2[i].astype(F32)

    cot = jnp.concatenate([left[:, 0:256], right], axis=1)
    own = x_ref[0, pl.ds(pl.multiple_of(16 * y, 16), 16), :].astype(F32)
    own_rms = jnp.sqrt(jnp.mean(own * own, axis=-1, keepdims=True) + 1e-06)
    xhat = own / own_rms
    scaled = gain_ref[...] * cot
    raw_ref[0] = (scaled - xhat * jnp.mean(scaled * xhat, axis=-1, keepdims=True)) / own_rms
    both = left[:, 256:384]
    rope_ref[0] = jnp.where(y >= ny // 2, pltpu.roll(both, 64, 1), both)[:, 0:64]

    gout_ref[...] = gain_sum(2) / gain_ref[...] * (1.0 / math.sqrt(total_rows))
    for copy in started:
        copy.wait_send()


def hand_over(raw_in, rope_in, gain_in, raw_out, rope_out, gain_out):
    raw_out[...] = raw_in[...]
    rope_out[...] = rope_in[...]
    gain_out[...] = gain_in[...]


def solution(mesh):
    nc, ny, nx = mesh.shape["ctx"], mesh.shape["head"], mesh.shape["dp"]
    nz = nc // 2
    half_z = nz // 2

    def per_device(pos, unnormed, gain, kr, qn, qr, ku, vu, go):
        dma = pltpu.SemaphoreType.DMA
        out = pl.pallas_call(
            functools.partial(kernel, nz, ny, nx, nc * 128 * nx),
            out_shape=(
                jax.ShapeDtypeStruct((1, 16, 512), F32),
                jax.ShapeDtypeStruct((1, 16, 64), F32),
                jax.ShapeDtypeStruct((1, 512), F32),
            ),
            in_specs=[pl.BlockSpec(memory_space=pltpu.HBM)] * 9,
            out_specs=[pl.BlockSpec(memory_space=pltpu.VMEM)] * 3,
            scratch_shapes=[
                pltpu.VMEM((1, 128), jnp.int32),
                pltpu.VMEM((1, 128, 512), BF16),
                pltpu.VMEM((1, 512), F32),
                pltpu.VMEM((1, 64, 128), BF16),
                pltpu.VMEM((1, 128, 1024), BF16),
                pltpu.VMEM((1, 128, 512), BF16),
                pltpu.VMEM((8, 128, 512), BF16),
                pltpu.VMEM((8, 128, 512), BF16),
                pltpu.VMEM((1, 128, 1024), BF16),
                dma((9,)),
                pltpu.VMEM((nc, 144, 512), BF16),
                pltpu.VMEM((nc, 1, 128), jnp.int32),
                pltpu.VMEM((2, 512, 512), BF16),
                pltpu.VMEM((2, 512, 512), BF16),
                pltpu.VMEM((3, 512, 128), BF16),
                pltpu.VMEM((3, 64 * nc, 512), F32),
                pltpu.VMEM((3, 64 * nc, 512), F32),
                pltpu.VMEM((64, 512), jnp.int32),
                pltpu.VMEM((nz, 288, 256), BF16),
                pltpu.VMEM((nz, 288, 256), BF16),
                pltpu.VMEM((nz, 288, 256), BF16),
                pltpu.VMEM((nz, 160, 256), BF16),
                pltpu.VMEM((nz, 160, 256), BF16),
                pltpu.VMEM((ny, nz, 16, 256), BF16),
                pltpu.VMEM((ny, nz, 16, 256), BF16),
                pltpu.VMEM((ny, 16, 384), BF16),
                pltpu.VMEM((ny, 16, 384), BF16),
                pltpu.VMEM((nz, 16, 256), BF16),
                pltpu.VMEM((nz, 16, 256), BF16),
                pltpu.VMEM((3, 1, 512), F32),
                pltpu.VMEM((nx, 1, 512), F32),
                pltpu.VMEM((ny, 1, 512), F32),
                pltpu.VMEM((nc, 1, 512), F32),
                dma((5, nz)),
                dma((5, nz)),
                dma((nc,)),
                dma((nc,)),
                dma((nz,)),
                dma((nz,)),
                dma((2, nz)),
                dma((2, nz)),
                dma((half_z + 2, ny)),
                dma((half_z + 2, ny)),
                dma((nx + ny + nc,)),
                dma((nx + ny + nc,)),
            ],
            compiler_params=pltpu.CompilerParams(
                collective_id=0, has_side_effects=True, vmem_limit_bytes=60 * 1024 * 1024
            ),
        )(pos, unnormed, gain.reshape(1, 512), jnp.swapaxes(kr, 1, 2), qn, qr, ku, vu, go)
        out = pl.pallas_call(
            hand_over,
            out_shape=tuple(jax.ShapeDtypeStruct(o.shape, F32) for o in out),
            in_specs=[pl.BlockSpec(memory_space=pltpu.VMEM)] * 3,
            out_specs=[pl.BlockSpec(memory_space=pltpu.VMEM)] * 3,
        )(*out)
        return out[0], out[1], out[2].reshape(512)

    in_specs = (
        P("dp", "ctx"),
        P("dp", "ctx", None),
        P(),
        P("dp", "ctx", None),
        P("dp", "ctx", "head"),
        P("dp", "ctx", "head"),
        P("head", None, None),
        P("head", None, None),
        P("dp", "ctx", "head"),
    )
    out_specs = (P("dp", ("ctx", "head"), None), P("dp", ("ctx", "head"), None), P())
    return jax.shard_map(
        per_device, mesh=mesh, in_specs=in_specs, out_specs=out_specs, check_vma=False
    )
```
